32 devices in a mesh: blk: 4 (over z), str: 8 (over y, x, core).
Axes of the slice: x: 2, y: 2, z: 4, core: 2. Of those that a mesh axis runs over, the one named last changes fastest.
Arguments:
- civec: bfloat16 [2048, 1024], P(('blk', 'str')), may hold values from -6 to 6
- beta_index: int32 [2, 50, 1024], replicated, may hold values from 0 to 1023
- beta_sign: int32 [2, 50, 1024], replicated, may hold values from -1 to 1
- alpha_index: int32 [2, 50, 2048], replicated, may hold values from 0 to 511
- alpha_sign: int32 [2, 50, 2048], replicated, may hold values from -1 to 1
- integrals: bfloat16 [2, 50, 50], replicated, may hold values from -0.078125 to 0.078125
- beta_operator: bfloat16 [1024, 1024], replicated, may hold values from -0.1875 to 0.1875
- alpha_operator: bfloat16 [2048, 512], P(('blk', 'str')), may hold values from -0.25 to 0.25
Outputs:
- sigma_out: float32 [2048, 1024], P(('blk', 'str'))
The draws below stay inside these ranges and needn't reach their ends.
All inputs are finite; a program needn't handle non-finite values.
Results may differ from the reference program's by a relative error of at most 0.0013.
Values may be sent and summed in bfloat16 or wider, within the bound.
No kernel may reach another device: no remote copies, remote signals or barrier semaphores. Data moves between devices by JAX's collectives and lax.ppermute only.
A program may use at most 128 MiB of HBM per device.

```python
import jax
import jax.numpy as jnp

A_DEV = 64
NB = 1024
PAIRS = 50
CLASSES = 2
ABLK = 512
NA = 2048
N_BLK = 4
N_STR = 8


def plant(entries, key, low, high):
    shape = entries.shape
    index_at = [jax.random.randint(jax.random.fold_in(key, axis), (), 0, shape[axis]) for axis in range(len(shape))]
    entries = entries.at[tuple(index_at)].set(low)
    longest = shape.index(max(shape))
    index_at[longest] = (index_at[longest] + 1) % shape[longest]
    return entries.at[tuple(index_at)].set(high)


def levels(key, extent, cuts, low, high):
    gain, own = 1.0, jax.random.fold_in(key, 6)
    for axis_at, parts in cuts:
        draws = jnp.exp(jax.random.uniform(jax.random.fold_in(own, axis_at), (parts,), jnp.float32, low / len(cuts), high / len(cuts)))
        gain = gain * jnp.repeat(draws, extent[axis_at] // parts).reshape([-1 if axis == axis_at else 1 for axis in range(len(extent))])
    return gain


def normal_values(stream_key, dims, deviation, reach, cuts=(), dtype=jnp.bfloat16):
    drawn = jax.random.normal(stream_key, dims, jnp.float32) * deviation
    if len(cuts) > 0:
        drawn = levels(stream_key, dims, cuts, -0.22, 0.18) * drawn
    return jnp.clip(drawn, min=-reach, max=reach).astype(dtype)


def setup_inputs(seed: int = 0) -> dict:
    splits = jax.random.split(jax.random.key(seed), 9)
    return {
        "civec": normal_values(splits[0], (NA, NB), 1.0, 6.0, ((0, 32),)),
        "beta_index": plant(jax.random.randint(splits[1], (CLASSES, PAIRS, NB), 0, NB), jax.random.fold_in(splits[1], 1), 0, NB - 1).astype(jnp.int32),
        "beta_sign": plant(jax.random.randint(splits[2], (CLASSES, PAIRS, NB), -1, 2), jax.random.fold_in(splits[2], 1), -1, 1).astype(jnp.int32),
        "alpha_index": plant(jax.random.randint(splits[3], (CLASSES, PAIRS, NA), 0, ABLK), jax.random.fold_in(splits[3], 1), 0, ABLK - 1).astype(jnp.int32),
        "alpha_sign": plant(jax.random.randint(splits[4], (CLASSES, PAIRS, NA), -1, 2), jax.random.fold_in(splits[4], 1), -1, 1).astype(jnp.int32),
        "integrals": normal_values(splits[5], (CLASSES, PAIRS, PAIRS), (PAIRS * PAIRS * CLASSES) ** -0.5, 0.078125),
        "beta_operator": normal_values(splits[6], (NB, NB), NB ** -0.5, 0.1875),
        "alpha_operator": normal_values(splits[7], (NA, ABLK), ABLK ** -0.5, 0.25, ((0, 32),)),
    }


def reference(civec, beta_index, beta_sign, alpha_index, alpha_sign, integrals, beta_operator, alpha_operator):
    block_rows = A_DEV * N_STR
    sign_beta = beta_sign.astype(jnp.float32)
    sign_alpha = alpha_sign.astype(jnp.float32)
    beta_term = jnp.dot(civec, beta_operator, preferred_element_type=jnp.float32)
    pieces = []
    for target in range(N_BLK):
        lower = target * block_rows
        upper = lower + block_rows
        partial_value = jnp.dot(alpha_operator[lower:upper], civec[lower:upper], preferred_element_type=jnp.float32)
        for symmetry in range(CLASSES):
            source_block = target ^ (1 << symmetry)
            source = civec[source_block * block_rows:(source_block + 1) * block_rows]
            coupled = jnp.take(source, beta_index[symmetry], axis=1).astype(jnp.float32) * sign_beta[symmetry][None]
            images = jnp.einsum('qp,apb->qab', integrals[symmetry].astype(jnp.float32), coupled).astype(jnp.bfloat16)
            row_index = alpha_index[symmetry][:, lower:upper].astype(jnp.int32)
            picked = jnp.take_along_axis(images, row_index[:, :, None], axis=1).astype(jnp.float32)
            partial_value = partial_value + jnp.sum(sign_alpha[symmetry][:, lower:upper][:, :, None] * picked, axis=0)
        pieces.append(partial_value)
    return beta_term + jnp.concatenate(pieces, axis=0)
```

```python
import functools

import jax
import jax.numpy as jnp
from jax import lax
from jax.experimental import pallas as pl
from jax.experimental.pallas import tpu as pltpu
from jax.sharding import PartitionSpec as P

QUAD = 4
STEP = 4 * QUAD
VMEM_LIMIT = 56 * 1024 * 1024


def whole():
    return pl.BlockSpec(memory_space=pltpu.VMEM)


def mixed_kernel(count, place_ref, *refs):
    pieces = refs[:count]
    onehot_ref, kron_ref, index_ref, sign_ref = refs[count : count + 4]
    outs = refs[count + 4 : 2 * count + 4]
    turned, images, total, ordered = refs[2 * count + 4 :]
    step = pl.program_id(0)
    block_rows = turned.shape[1]
    local_rows = pieces[0].shape[0]
    halves = images.shape[0]
    group = kron_ref.shape[0]

    @pl.when(step == 0)
    def _():
        for at in range(0, count, 2):
            both = jnp.concatenate([pieces[at][...], pieces[at + 1][...]], axis=0)
            turned[:, at * local_rows : (at + 2) * local_rows] = both.T

    coupled = jnp.dot(onehot_ref[...], turned[...], preferred_element_type=jnp.float32)
    coupled = coupled.astype(jnp.bfloat16)
    low = lax.broadcasted_iota(jnp.int32, (halves, 8, block_rows), 1) < QUAD
    evens, odds = [], []
    for pair in range(2):
        first, second = [
            jnp.dot(
                kron_ref[...],
                coupled[at * group : (at + 1) * group],
                preferred_element_type=jnp.float32,
            ).reshape(halves, 8, block_rows)
            for at in (2 * pair, 2 * pair + 1)
        ]
        evens.append(jnp.where(low, first, pltpu.roll(second, QUAD, 1)))
        odds.append(jnp.where(low, pltpu.roll(first, QUAD, 1), second))
    rows = pl.ds(pl.multiple_of(step * STEP, STEP), STEP)
    images[:, 0, rows, :] = jnp.concatenate(evens, axis=1).astype(jnp.bfloat16)
    images[:, 1, rows, :] = jnp.concatenate(odds, axis=1).astype(jnp.bfloat16)

    @pl.when(step == pl.num_programs(0) - 1)
    def _():
        total[...] = jnp.zeros_like(total)
        position = lax.broadcasted_iota(jnp.int32, (block_rows, block_rows), 0)

        def body(half, carry):
            terms = []
            for side in range(2):
                pair = 2 * half + side
                selector = jnp.where(
                    position == index_ref[pl.ds(pair, 1), :], sign_ref[pl.ds(pair, 1), :], 0.0
                ).astype(jnp.bfloat16)
                terms.append(
                    jnp.dot(images[half, side], selector, preferred_element_type=jnp.float32)
                )
            total[...] += terms[0] + terms[1]
            return carry

        lax.fori_loop(0, halves, body, 0)
        ordered[...] = total[...].T
        for at in range(count):
            start = pl.multiple_of((place_ref[0] ^ at) * local_rows, local_rows)
            outs[at][...] = ordered[pl.ds(start, local_rows), :]


def mixed_pieces(place, pieces, onehot, kron, index, sign, window):
    count = len(pieces)
    local_rows, beta_count = pieces[0].shape
    pair_count, block_rows = index.shape
    steps = window // STEP
    rows = pair_count * STEP
    flops = 2 * window * pair_count * block_rows * (beta_count + pair_count * QUAD + block_rows)
    return pl.pallas_call(
        functools.partial(mixed_kernel, count),
        out_shape=[jax.ShapeDtypeStruct((local_rows, window), jnp.float32)] * count,
        grid_spec=pltpu.PrefetchScalarGridSpec(
            num_scalar_prefetch=1,
            grid=(steps,),
            in_specs=[whole()] * count
            + [pl.BlockSpec((rows, beta_count), lambda i, place_ref: (i, 0))]
            + [whole()] * 3,
            out_specs=[whole()] * count,
            scratch_shapes=[
                pltpu.VMEM((beta_count, block_rows), jnp.bfloat16),
                pltpu.VMEM((pair_count // 2, 2, window, block_rows), jnp.bfloat16),
                pltpu.VMEM((window, block_rows), jnp.float32),
                pltpu.VMEM((block_rows, window), jnp.float32),
            ],
        ),
        compiler_params=pltpu.CompilerParams(
            dimension_semantics=("arbitrary",), vmem_limit_bytes=VMEM_LIMIT
        ),
        cost_estimate=pl.CostEstimate(
            flops=flops, bytes_accessed=2 * onehot.size, transcendentals=0
        ),
        name="mixed",
    )(place, *pieces, onehot, kron, index, sign)


def plain_kernel(count, place_ref, *refs):
    pieces = refs[:count]
    alpha_ref, beta_ref, out_ref, block = refs[count:]
    local_rows = pieces[0].shape[0]
    for at in range(count):
        start = pl.multiple_of((place_ref[0] ^ at) * local_rows, local_rows)
        block[pl.ds(start, local_rows), :] = pieces[at][...]
    out_ref[...] = jnp.dot(
        alpha_ref[...], block[...], preferred_element_type=jnp.float32
    ) + jnp.dot(pieces[0][...], beta_ref[...], preferred_element_type=jnp.float32)


def plain_terms(place, pieces, alpha_operator, beta_operator):
    count = len(pieces)
    local_rows, beta_count = pieces[0].shape
    block_rows = alpha_operator.shape[1]
    return pl.pallas_call(
        functools.partial(plain_kernel, count),
        out_shape=jax.ShapeDtypeStruct((local_rows, beta_count), jnp.float32),
        in_specs=[pl.BlockSpec(memory_space=pltpu.SMEM)] + [whole()] * (count + 2),
        out_specs=whole(),
        scratch_shapes=[pltpu.VMEM((block_rows, beta_count), jnp.bfloat16)],
        compiler_params=pltpu.CompilerParams(vmem_limit_bytes=VMEM_LIMIT),
        cost_estimate=pl.CostEstimate(
            flops=2 * local_rows * beta_count * (beta_count + block_rows),
            bytes_accessed=2 * beta_count * (beta_count + block_rows),
            transcendentals=0,
        ),
        name="plain",
    )(place, *pieces, alpha_operator, beta_operator)


def add_kernel(count, classes, place_ref, base_ref, *refs):
    terms, out_ref = refs[:count], refs[count]
    window = terms[0].shape[1]
    chunk = place_ref[0] // classes
    for at in range(0, count, classes):
        start = pl.multiple_of((chunk ^ (at // classes)) * window, window)
        columns = pl.ds(start, window)
        value = base_ref[:, columns]
        for other in range(classes):
            value = value + terms[at + other][...]
        out_ref[:, columns] = value


def add_terms(place, base, terms, classes):
    count = len(terms)
    return pl.pallas_call(
        functools.partial(add_kernel, count, classes),
        out_shape=jax.ShapeDtypeStruct(base.shape, jnp.float32),
        in_specs=[pl.BlockSpec(memory_space=pltpu.SMEM)] + [whole()] * (count + 1),
        out_specs=whole(),
        compiler_params=pltpu.CompilerParams(vmem_limit_bytes=VMEM_LIMIT),
        name="add",
    )(place, base, *terms)


def local(
    civec, beta_index, beta_sign, alpha_index, alpha_sign, integrals, beta_operator, alpha_operator
):
    classes, pair_count = integrals.shape[:2]
    local_rows, beta_count = civec.shape
    count = lax.axis_size("str")
    blocks = lax.axis_size("blk")
    block_rows = local_rows * count
    window = beta_count * classes // count
    quads = window // QUAD
    block_at, place = lax.axis_index("blk"), lax.axis_index("str")
    symmetry, chunk = place % classes, place // classes
    scalar_place = place.astype(jnp.int32).reshape(1)

    def near(array, distance):
        route = [
            (blk * count + at, blk * count + (at ^ distance))
            for blk in range(blocks)
            for at in range(count)
        ]
        return lax.ppermute(array, ("blk", "str"), route)

    def far(array, distance):
        route = [
            (blk * count + at, (blk ^ (1 << at % classes)) * count + (at ^ distance))
            for blk in range(blocks)
            for at in range(count)
        ]
        return lax.ppermute(array, ("blk", "str"), route)

    straight = [civec] + [near(civec, at) for at in range(2, count, 2)]
    crossed = [near(piece, 1) for piece in straight]
    pieces = [piece for two in zip(straight, crossed) for piece in two]

    def one_class(array, start, width):
        return lax.dynamic_slice(array, (symmetry, 0, start), (1, array.shape[1], width))[0]

    def by_quad(array):
        part = one_class(array, chunk * window, window).reshape(pair_count, quads, QUAD)
        return part.transpose(1, 0, 2).reshape(pair_count * window, 1)

    positions = jnp.arange(beta_count, dtype=jnp.int32)[None, :]
    onehot = jnp.where(by_quad(beta_index) == positions, by_quad(beta_sign), 0).astype(jnp.bfloat16)
    same = jnp.eye(QUAD, dtype=jnp.bfloat16)
    own_integrals = lax.dynamic_index_in_dim(integrals, symmetry, 0, keepdims=False)
    kron = (own_integrals[:, None, :, None] * same[None, :, None, :]).reshape(
        pair_count * QUAD, pair_count * QUAD
    )
    partner = jnp.bitwise_xor(block_at, 1 << symmetry)
    index = one_class(alpha_index, partner * block_rows, block_rows)
    index = jnp.bitwise_xor(index // local_rows, place) * local_rows + index % local_rows
    sign = one_class(alpha_sign, partner * block_rows, block_rows).astype(jnp.float32)

    sent = mixed_pieces(scalar_place, pieces, onehot, kron, index, sign, window)
    terms = [far(sent[at], at) for at in range(count)]
    base = plain_terms(scalar_place, pieces, alpha_operator, beta_operator)
    return add_terms(scalar_place, base, terms, classes)


def solution(mesh):
    placed = (P(("blk", "str"), None), P(), P(), P(), P(), P(), P(), P(("blk", "str"), None))
    return jax.shard_map(
        local, mesh=mesh, in_specs=placed, out_specs=P(("blk", "str"), None), check_vma=False
    )
```

```python
import functools

import jax
import jax.numpy as jnp
from jax import lax
from jax.experimental import pallas as pl
from jax.experimental.pallas import tpu as pltpu
from jax.sharding import PartitionSpec as P

QUAD = 4
VMEM_LIMIT = 56 * 1024 * 1024


def whole():
    return pl.BlockSpec(memory_space=pltpu.VMEM)


def prepare_kernel(place_ref, index_ref, sign_ref, integral_ref, code_ref, kron_ref):
    pairs, window = index_ref.shape[1:]
    codes = index_ref[0] * 4 + sign_ref[0] + 1
    low = lax.broadcasted_iota(jnp.int32, (128 // 8, 8, 128), 1) < QUAD
    for start in range(0, window, 128):
        for half in range(pairs // 2):
            first, second = [
                jnp.broadcast_to(codes[pair : pair + 1, start : start + 128], (128, 128))
                .T.reshape(128 // 8, 8, 128)
                for pair in (2 * half, 2 * half + 1)
            ]
            rows = slice(start // 8, (start + 128) // 8)
            code_ref[rows, 0, half] = jnp.where(low, first, pltpu.roll(second, QUAD, 1))
            code_ref[rows, 1, half] = jnp.where(low, pltpu.roll(first, QUAD, 1), second)
    size = pairs * QUAD
    spread = (
        lax.broadcasted_iota(jnp.int32, (size, pairs), 0) // QUAD
        == lax.broadcasted_iota(jnp.int32, (size, pairs), 1)
    ).astype(jnp.bfloat16)
    tall = jnp.dot(spread, integral_ref[0], preferred_element_type=jnp.float32)
    wide = lax.dot_general(
        tall.astype(jnp.bfloat16),
        spread,
        (((1,), (1,)), ((), ())),
        preferred_element_type=jnp.float32,
    )
    row = lax.broadcasted_iota(jnp.int32, (size, size), 0)
    column = lax.broadcasted_iota(jnp.int32, (size, size), 1)
    kron_ref[...] = jnp.where(row % QUAD == column % QUAD, wide, 0.0).astype(jnp.bfloat16)


def prepare(place, beta_index, beta_sign, integrals, window):
    pairs = beta_index.shape[1]
    size = pairs * QUAD
    part = pl.BlockSpec((1, pairs, window), lambda i, at: (at[1], 0, at[2]))
    codes, kron = pl.pallas_call(
        prepare_kernel,
        out_shape=[
            jax.ShapeDtypeStruct((window // 8, 2, pairs // 2, 8, 128), jnp.int32),
            jax.ShapeDtypeStruct((size, size), jnp.bfloat16),
        ],
        grid_spec=pltpu.PrefetchScalarGridSpec(
            num_scalar_prefetch=1,
            grid=(1,),
            in_specs=[part, part, pl.BlockSpec((1, pairs, pairs), lambda i, at: (at[1], 0, 0))],
            out_specs=[whole(), whole()],
        ),
        compiler_params=pltpu.CompilerParams(vmem_limit_bytes=VMEM_LIMIT),
        cost_estimate=pl.CostEstimate(
            flops=0, bytes_accessed=4 * window * size * 32, transcendentals=0
        ),
        name="prepare",
    )(place, beta_index, beta_sign, integrals)
    return codes.reshape(window * pairs, 128), kron


def mixed_kernel(count, bundle, place_ref, *refs):
    pieces = refs[:count]
    code_ref, kron_ref, index_ref, sign_ref = refs[count : count + 4]
    outs = refs[count + 4 : 2 * count + 4]
    turned, images, total, ordered, signs = refs[2 * count + 4 :]
    step = pl.program_id(0)
    beta_count, block_rows = turned.shape
    local_rows = pieces[0].shape[0]
    halves = images.shape[0]
    group = kron_ref.shape[0]
    rows = code_ref.shape[0]
    quads = rows // group

    @pl.when(step == 0)
    def _():
        for at in range(0, count, 2):
            both = jnp.concatenate([pieces[at][...], pieces[at + 1][...]], axis=0)
            turned[:, at * local_rows : (at + 2) * local_rows] = both.T

    codes = code_ref[...]
    target = jnp.right_shift(codes, 2)
    value = ((codes & 3) - 1).astype(jnp.float32)
    lane = lax.broadcasted_iota(jnp.int32, (rows, 128), 1)
    onehot = jnp.concatenate(
        [
            jnp.where(lane == target - start, value, 0.0).astype(jnp.bfloat16)
            for start in range(0, beta_count, 128)
        ],
        axis=1,
    )
    coupled = jnp.dot(onehot, turned[...], preferred_element_type=jnp.float32)
    coupled = coupled.astype(jnp.bfloat16)
    low = lax.broadcasted_iota(jnp.int32, (halves, 8, block_rows), 1) < QUAD
    evens, odds = [], []
    for pair in range(quads // 2):
        first, second = [
            jnp.dot(
                kron_ref[...],
                coupled[at * group : (at + 1) * group],
                preferred_element_type=jnp.float32,
            ).reshape(halves, 8, block_rows)
            for at in (2 * pair, 2 * pair + 1)
        ]
        evens.append(jnp.where(low, first, pltpu.roll(second, QUAD, 1)))
        odds.append(jnp.where(low, pltpu.roll(first, QUAD, 1), second))
    columns = quads * QUAD
    place = pl.ds(pl.multiple_of(step * columns, columns), columns)
    images[:, 0, place, :] = jnp.concatenate(evens, axis=1).astype(jnp.bfloat16)
    images[:, 1, place, :] = jnp.concatenate(odds, axis=1).astype(jnp.bfloat16)

    @pl.when(step == pl.num_programs(0) - 1)
    def _():
        total[...] = jnp.zeros_like(total)
        signs[...] = sign_ref[0].astype(jnp.float32)
        position = lax.broadcasted_iota(jnp.int32, (block_rows, block_rows), 0)
        position = jnp.bitwise_xor(position, place_ref[0] * local_rows)

        def body(at, carry):
            term = None
            for offset in range(bundle):
                pair = bundle * at + offset
                selector = jnp.where(
                    position == index_ref[0, pl.ds(pair, 1), :], signs[pl.ds(pair, 1), :], 0.0
                ).astype(jnp.bfloat16)
                part = jnp.dot(
                    images[lax.div(pair, 2), lax.rem(pair, 2)],
                    selector,
                    preferred_element_type=jnp.float32,
                )
                term = part if term is None else term + part
            total[...] += term
            return carry

        lax.fori_loop(0, 2 * halves // bundle, body, 0)
        ordered[...] = total[...].T
        for at in range(count):
            start = pl.multiple_of((place_ref[0] ^ at) * local_rows, local_rows)
            outs[at][...] = ordered[pl.ds(start, local_rows), :]


def mixed_pieces(place, pieces, codes, kron, alpha_index, alpha_sign, window):
    count = len(pieces)
    local_rows, beta_count = pieces[0].shape
    pairs = alpha_index.shape[1]
    block_rows = count * local_rows
    columns = min(64, window)
    rows = pairs * columns
    bundle = next(size for size in (10, 5, 2, 1) if pairs % size == 0)
    flops = 2 * window * pairs * block_rows * (beta_count + pairs * QUAD + block_rows)
    part = pl.BlockSpec((1, pairs, block_rows), lambda i, at: (at[1], 0, at[3]))
    return pl.pallas_call(
        functools.partial(mixed_kernel, count, bundle),
        out_shape=[jax.ShapeDtypeStruct((local_rows, window), jnp.float32)] * count,
        grid_spec=pltpu.PrefetchScalarGridSpec(
            num_scalar_prefetch=1,
            grid=(window // columns,),
            in_specs=[whole()] * count
            + [pl.BlockSpec((rows, 128), lambda i, at: (i, 0)), whole(), part, part],
            out_specs=[whole()] * count,
            scratch_shapes=[
                pltpu.VMEM((beta_count, block_rows), jnp.bfloat16),
                pltpu.VMEM((pairs // 2, 2, window, block_rows), jnp.bfloat16),
                pltpu.VMEM((window, block_rows), jnp.float32),
                pltpu.VMEM((block_rows, window), jnp.float32),
                pltpu.VMEM((pairs, block_rows), jnp.float32),
            ],
        ),
        compiler_params=pltpu.CompilerParams(
            dimension_semantics=("arbitrary",), vmem_limit_bytes=VMEM_LIMIT
        ),
        cost_estimate=pl.CostEstimate(
            flops=flops, bytes_accessed=4 * codes.size, transcendentals=0
        ),
        name="mixed",
    )(place, *pieces, codes, kron, alpha_index, alpha_sign)


def plain_kernel(count, place_ref, *refs):
    pieces = refs[:count]
    alpha_ref, beta_ref, out_ref, block = refs[count:]
    local_rows = pieces[0].shape[0]
    for at in range(count):
        start = pl.multiple_of((place_ref[0] ^ at) * local_rows, local_rows)
        block[pl.ds(start, local_rows), :] = pieces[at][...]
    out_ref[...] = jnp.dot(
        alpha_ref[...], block[...], preferred_element_type=jnp.float32
    ) + jnp.dot(pieces[0][...], beta_ref[...], preferred_element_type=jnp.float32)


def plain_terms(place, pieces, alpha_operator, beta_operator):
    count = len(pieces)
    local_rows, beta_count = pieces[0].shape
    block_rows = alpha_operator.shape[1]
    return pl.pallas_call(
        functools.partial(plain_kernel, count),
        out_shape=jax.ShapeDtypeStruct((local_rows, beta_count), jnp.float32),
        in_specs=[pl.BlockSpec(memory_space=pltpu.SMEM)] + [whole()] * (count + 2),
        out_specs=whole(),
        scratch_shapes=[pltpu.VMEM((block_rows, beta_count), jnp.bfloat16)],
        compiler_params=pltpu.CompilerParams(vmem_limit_bytes=VMEM_LIMIT),
        cost_estimate=pl.CostEstimate(
            flops=2 * local_rows * beta_count * (beta_count + block_rows),
            bytes_accessed=2 * beta_count * (beta_count + block_rows),
            transcendentals=0,
        ),
        name="plain",
    )(place, *pieces, alpha_operator, beta_operator)


def add_kernel(count, classes, place_ref, base_ref, *refs):
    terms, out_ref = refs[:count], refs[count]
    window = terms[0].shape[1]
    chunk = place_ref[0] // classes
    for at in range(0, count, classes):
        start = pl.multiple_of((chunk ^ (at // classes)) * window, window)
        columns = pl.ds(start, window)
        value = base_ref[:, columns]
        for other in range(classes):
            value = value + terms[at + other][...]
        out_ref[:, columns] = value


def add_terms(place, base, terms, classes):
    count = len(terms)
    return pl.pallas_call(
        functools.partial(add_kernel, count, classes),
        out_shape=jax.ShapeDtypeStruct(base.shape, jnp.float32),
        in_specs=[pl.BlockSpec(memory_space=pltpu.SMEM)] + [whole()] * (count + 1),
        out_specs=whole(),
        compiler_params=pltpu.CompilerParams(vmem_limit_bytes=VMEM_LIMIT),
        name="add",
    )(place, base, *terms)


def local(
    civec, beta_index, beta_sign, alpha_index, alpha_sign, integrals, beta_operator, alpha_operator
):
    classes, pair_count = integrals.shape[:2]
    local_rows, beta_count = civec.shape
    count = lax.axis_size("str")
    blocks = lax.axis_size("blk")
    block_rows = local_rows * count
    window = beta_count * classes // count
    block_at, place = lax.axis_index("blk"), lax.axis_index("str")
    symmetry = place % classes
    partner = jnp.bitwise_xor(block_at, 1 << symmetry)
    place = jnp.stack([place, symmetry, place // classes, partner]).astype(jnp.int32)

    def near(array, distance):
        route = [
            (blk * count + at, blk * count + (at ^ distance))
            for blk in range(blocks)
            for at in range(count)
        ]
        return lax.ppermute(array, ("blk", "str"), route)

    def far(array, distance):
        route = [
            (blk * count + at, (blk ^ (1 << at % classes)) * count + (at ^ distance))
            for blk in range(blocks)
            for at in range(count)
        ]
        return lax.ppermute(array, ("blk", "str"), route)

    straight = [civec] + [near(civec, at) for at in range(2, count, 2)]
    crossed = [near(piece, 1) for piece in straight]
    pieces = [piece for two in zip(straight, crossed) for piece in two]

    codes, kron = prepare(place, beta_index, beta_sign, integrals, window)
    sent = mixed_pieces(place, pieces, codes, kron, alpha_index, alpha_sign, window)
    terms = [far(sent[at], at) for at in range(count)]
    base = plain_terms(place, pieces, alpha_operator, beta_operator)
    return add_terms(place, base, terms, classes)


def solution(mesh):
    placed = (P(("blk", "str"), None), P(), P(), P(), P(), P(), P(), P(("blk", "str"), None))
    return jax.shard_map(
        local, mesh=mesh, in_specs=placed, out_specs=P(("blk", "str"), None), check_vma=False
    )
```

```python
import functools

import jax
import jax.numpy as jnp
from jax import lax
from jax.experimental import pallas as pl
from jax.experimental.pallas import tpu as pltpu
from jax.sharding import PartitionSpec as P

QUAD = 4
VMEM_LIMIT = 56 * 1024 * 1024


def whole():
    return pl.BlockSpec(memory_space=pltpu.VMEM)


def of_class(values, symmetry):
    picked = values[:, 0, :]
    for other in range(1, values.shape[1]):
        picked = jnp.where(symmetry == other, values[:, other, :], picked)
    return picked


def prepare_kernel(place_ref, index_ref, sign_ref, integral_ref, code_ref, kron_ref):
    pairs, _, window = index_ref.shape
    codes = of_class(index_ref[...] * 4 + sign_ref[...] + 1, place_ref[1])
    integrals = of_class(integral_ref[...].astype(jnp.float32), place_ref[1])
    low = lax.broadcasted_iota(jnp.int32, (128 // 8, 8, 128), 1) < QUAD
    for start in range(0, window, 128):
        for half in range(pairs // 2):
            first, second = [
                jnp.broadcast_to(codes[pair : pair + 1, start : start + 128], (128, 128))
                .T.reshape(128 // 8, 8, 128)
                for pair in (2 * half, 2 * half + 1)
            ]
            rows = slice(start // 8, (start + 128) // 8)
            code_ref[rows, 0, half] = jnp.where(low, first, pltpu.roll(second, QUAD, 1))
            code_ref[rows, 1, half] = jnp.where(low, pltpu.roll(first, QUAD, 1), second)
    size = pairs * QUAD
    spread = (
        lax.broadcasted_iota(jnp.int32, (size, pairs), 0) // QUAD
        == lax.broadcasted_iota(jnp.int32, (size, pairs), 1)
    ).astype(jnp.bfloat16)
    tall = jnp.dot(spread, integrals.astype(jnp.bfloat16), preferred_element_type=jnp.float32)
    wide = lax.dot_general(
        tall.astype(jnp.bfloat16),
        spread,
        (((1,), (1,)), ((), ())),
        preferred_element_type=jnp.float32,
    )
    row = lax.broadcasted_iota(jnp.int32, (size, size), 0)
    column = lax.broadcasted_iota(jnp.int32, (size, size), 1)
    kron_ref[...] = jnp.where(row % QUAD == column % QUAD, wide, 0.0).astype(jnp.bfloat16)


def prepare(place, beta_index, beta_sign, integrals, window):
    pairs, classes = beta_index.shape[:2]
    size = pairs * QUAD
    part = pl.BlockSpec((pairs, classes, window), lambda i, at: (0, 0, at[2]))
    codes, kron = pl.pallas_call(
        prepare_kernel,
        out_shape=[
            jax.ShapeDtypeStruct((window // 8, 2, pairs // 2, 8, 128), jnp.int32),
            jax.ShapeDtypeStruct((size, size), jnp.bfloat16),
        ],
        grid_spec=pltpu.PrefetchScalarGridSpec(
            num_scalar_prefetch=1,
            grid=(1,),
            in_specs=[part, part, whole()],
            out_specs=[whole(), whole()],
        ),
        compiler_params=pltpu.CompilerParams(vmem_limit_bytes=VMEM_LIMIT),
        cost_estimate=pl.CostEstimate(
            flops=0, bytes_accessed=4 * window * size * 32, transcendentals=0
        ),
        name="prepare",
    )(place, beta_index, beta_sign, integrals)
    return codes.reshape(window * pairs, 128), kron


def mixed_kernel(count, bundle, place_ref, *refs):
    pieces = refs[:count]
    code_ref, kron_ref, index_ref, sign_ref = refs[count : count + 4]
    outs = refs[count + 4 : 2 * count + 4]
    turned, images, total, ordered, indices, signs = refs[2 * count + 4 :]
    step = pl.program_id(0)
    beta_count, block_rows = turned.shape
    local_rows = pieces[0].shape[0]
    halves = images.shape[0]
    group = kron_ref.shape[0]
    rows = code_ref.shape[0]
    quads = rows // group

    @pl.when(step == 0)
    def _():
        for at in range(0, count, 2):
            both = jnp.concatenate([pieces[at][...], pieces[at + 1][...]], axis=0)
            turned[:, at * local_rows : (at + 2) * local_rows] = both.T

    codes = code_ref[...]
    target = jnp.right_shift(codes, 2)
    value = ((codes & 3) - 1).astype(jnp.float32)
    lane = lax.broadcasted_iota(jnp.int32, (rows, 128), 1)
    onehot = jnp.concatenate(
        [
            jnp.where(lane == target - start, value, 0.0).astype(jnp.bfloat16)
            for start in range(0, beta_count, 128)
        ],
        axis=1,
    )
    coupled = jnp.dot(onehot, turned[...], preferred_element_type=jnp.float32)
    coupled = coupled.astype(jnp.bfloat16)
    low = lax.broadcasted_iota(jnp.int32, (halves, 8, block_rows), 1) < QUAD
    evens, odds = [], []
    for pair in range(quads // 2):
        first, second = [
            jnp.dot(
                kron_ref[...],
                coupled[at * group : (at + 1) * group],
                preferred_element_type=jnp.float32,
            ).reshape(halves, 8, block_rows)
            for at in (2 * pair, 2 * pair + 1)
        ]
        evens.append(jnp.where(low, first, pltpu.roll(second, QUAD, 1)))
        odds.append(jnp.where(low, pltpu.roll(first, QUAD, 1), second))
    columns = quads * QUAD
    place = pl.ds(pl.multiple_of(step * columns, columns), columns)
    images[:, 0, place, :] = jnp.concatenate(evens, axis=1).astype(jnp.bfloat16)
    images[:, 1, place, :] = jnp.concatenate(odds, axis=1).astype(jnp.bfloat16)

    @pl.when(step == pl.num_programs(0) - 1)
    def _():
        total[...] = jnp.zeros_like(total)
        indices[...] = of_class(index_ref[...], place_ref[1])
        signs[...] = of_class(sign_ref[...], place_ref[1]).astype(jnp.float32)
        position = lax.broadcasted_iota(jnp.int32, (block_rows, block_rows), 0)
        position = jnp.bitwise_xor(position, place_ref[0] * local_rows)

        def body(at, carry):
            term = None
            for offset in range(bundle):
                pair = bundle * at + offset
                selector = jnp.where(
                    position == indices[pl.ds(pair, 1), :], signs[pl.ds(pair, 1), :], 0.0
                ).astype(jnp.bfloat16)
                part = jnp.dot(
                    images[lax.div(pair, 2), lax.rem(pair, 2)],
                    selector,
                    preferred_element_type=jnp.float32,
                )
                term = part if term is None else term + part
            total[...] += term
            return carry

        lax.fori_loop(0, 2 * halves // bundle, body, 0)
        ordered[...] = total[...].T
        for at in range(count):
            start = pl.multiple_of((place_ref[0] ^ at) * local_rows, local_rows)
            outs[at][...] = ordered[pl.ds(start, local_rows), :]


def mixed_pieces(place, pieces, codes, kron, alpha_index, alpha_sign, window):
    count = len(pieces)
    local_rows, beta_count = pieces[0].shape
    pairs, classes = alpha_index.shape[:2]
    block_rows = count * local_rows
    columns = min(64, window)
    rows = pairs * columns
    bundle = next(size for size in (10, 5, 2, 1) if pairs % size == 0)
    flops = 2 * window * pairs * block_rows * (beta_count + pairs * QUAD + block_rows)
    part = pl.BlockSpec((pairs, classes, block_rows), lambda i, at: (0, 0, at[3]))
    return pl.pallas_call(
        functools.partial(mixed_kernel, count, bundle),
        out_shape=[jax.ShapeDtypeStruct((local_rows, window), jnp.float32)] * count,
        grid_spec=pltpu.PrefetchScalarGridSpec(
            num_scalar_prefetch=1,
            grid=(window // columns,),
            in_specs=[whole()] * count
            + [pl.BlockSpec((rows, 128), lambda i, at: (i, 0)), whole(), part, part],
            out_specs=[whole()] * count,
            scratch_shapes=[
                pltpu.VMEM((beta_count, block_rows), jnp.bfloat16),
                pltpu.VMEM((pairs // 2, 2, window, block_rows), jnp.bfloat16),
                pltpu.VMEM((window, block_rows), jnp.float32),
                pltpu.VMEM((block_rows, window), jnp.float32),
                pltpu.VMEM((pairs, block_rows), jnp.int32),
                pltpu.VMEM((pairs, block_rows), jnp.float32),
            ],
        ),
        compiler_params=pltpu.CompilerParams(
            dimension_semantics=("arbitrary",), vmem_limit_bytes=VMEM_LIMIT
        ),
        cost_estimate=pl.CostEstimate(
            flops=flops, bytes_accessed=4 * codes.size, transcendentals=0
        ),
        name="mixed",
    )(place, *pieces, codes, kron, alpha_index, alpha_sign)


def plain_kernel(count, place_ref, *refs):
    pieces = refs[:count]
    alpha_ref, beta_ref, out_ref, block = refs[count:]
    local_rows = pieces[0].shape[0]
    for at in range(count):
        start = pl.multiple_of((place_ref[0] ^ at) * local_rows, local_rows)
        block[pl.ds(start, local_rows), :] = pieces[at][...]
    out_ref[...] = jnp.dot(
        alpha_ref[...], block[...], preferred_element_type=jnp.float32
    ) + jnp.dot(pieces[0][...], beta_ref[...], preferred_element_type=jnp.float32)


def plain_terms(place, pieces, alpha_operator, beta_operator):
    count = len(pieces)
    local_rows, beta_count = pieces[0].shape
    block_rows = alpha_operator.shape[1]
    return pl.pallas_call(
        functools.partial(plain_kernel, count),
        out_shape=jax.ShapeDtypeStruct((local_rows, beta_count), jnp.float32),
        in_specs=[pl.BlockSpec(memory_space=pltpu.SMEM)] + [whole()] * (count + 2),
        out_specs=whole(),
        scratch_shapes=[pltpu.VMEM((block_rows, beta_count), jnp.bfloat16)],
        compiler_params=pltpu.CompilerParams(vmem_limit_bytes=VMEM_LIMIT),
        cost_estimate=pl.CostEstimate(
            flops=2 * local_rows * beta_count * (beta_count + block_rows),
            bytes_accessed=2 * beta_count * (beta_count + block_rows),
            transcendentals=0,
        ),
        name="plain",
    )(place, *pieces, alpha_operator, beta_operator)


def add_kernel(count, classes, place_ref, base_ref, *refs):
    terms, out_ref = refs[:count], refs[count]
    window = terms[0].shape[1]
    chunk = place_ref[0] // classes
    for at in range(0, count, classes):
        start = pl.multiple_of((chunk ^ (at // classes)) * window, window)
        columns = pl.ds(start, window)
        value = base_ref[:, columns]
        for other in range(classes):
            value = value + terms[at + other][...]
        out_ref[:, columns] = value


def add_terms(place, base, terms, classes):
    count = len(terms)
    return pl.pallas_call(
        functools.partial(add_kernel, count, classes),
        out_shape=jax.ShapeDtypeStruct(base.shape, jnp.float32),
        in_specs=[pl.BlockSpec(memory_space=pltpu.SMEM)] + [whole()] * (count + 1),
        out_specs=whole(),
        compiler_params=pltpu.CompilerParams(vmem_limit_bytes=VMEM_LIMIT),
        name="add",
    )(place, base, *terms)


def local(
    civec, beta_index, beta_sign, alpha_index, alpha_sign, integrals, beta_operator, alpha_operator
):
    classes, pair_count = integrals.shape[:2]
    local_rows, beta_count = civec.shape
    count = lax.axis_size("str")
    blocks = lax.axis_size("blk")
    block_rows = local_rows * count
    window = beta_count * classes // count
    block_at, place = lax.axis_index("blk"), lax.axis_index("str")
    symmetry = place % classes
    partner = jnp.bitwise_xor(block_at, 1 << symmetry)
    place = jnp.stack([place, symmetry, place // classes, partner]).astype(jnp.int32)

    def near(array, distance):
        route = [
            (blk * count + at, blk * count + (at ^ distance))
            for blk in range(blocks)
            for at in range(count)
        ]
        return lax.ppermute(array, ("blk", "str"), route)

    def far(array, distance):
        route = [
            (blk * count + at, (blk ^ (1 << at % classes)) * count + (at ^ distance))
            for blk in range(blocks)
            for at in range(count)
        ]
        return lax.ppermute(array, ("blk", "str"), route)

    by_pair = [
        jnp.transpose(array, (1, 0, 2))
        for array in (beta_index, beta_sign, integrals, alpha_index, alpha_sign)
    ]
    arrived = [near(civec, at) for at in range(2, count, 2)]
    codes, kron = prepare(place, *by_pair[:3], window)
    codes, kron, *arrived = lax.optimization_barrier((codes, kron, *arrived))
    straight = [civec] + arrived
    crossed = [near(piece, 1) for piece in straight]
    pieces = [piece for two in zip(straight, crossed) for piece in two]

    sent = mixed_pieces(place, pieces, codes, kron, *by_pair[3:], window)
    terms = [far(sent[at], at) for at in range(count)]
    base = plain_terms(place, pieces, alpha_operator, beta_operator)
    return add_terms(place, base, terms, classes)


def solution(mesh):
    placed = (P(("blk", "str"), None), P(), P(), P(), P(), P(), P(), P(("blk", "str"), None))
    return jax.shard_map(
        local, mesh=mesh, in_specs=placed, out_specs=P(("blk", "str"), None), check_vma=False
    )
```

```python
import functools

import jax
import jax.numpy as jnp
from jax import lax
from jax.experimental import pallas as pl
from jax.experimental.pallas import tpu as pltpu
from jax.sharding import PartitionSpec as P

QUAD = 4
VMEM_LIMIT = 46 * 1024 * 1024


def whole():
    return pl.BlockSpec(memory_space=pltpu.VMEM)


def any_place():
    return pl.BlockSpec(memory_space=pl.ANY)


def in_hbm():
    return pl.BlockSpec(memory_space=pltpu.HBM)


def prepare_kernel(code_ref, integral_ref, rows_ref, out_ref, kron_ref, copied_ref, arrived):
    pairs, window = code_ref.shape
    quads = window // QUAD
    size = pairs * QUAD
    copy = pltpu.make_async_copy(rows_ref, copied_ref, arrived)
    copy.start()
    codes = code_ref[...]
    for part in range(QUAD):
        out_ref[pl.ds(part, pairs, QUAD), :quads] = codes[:, part * quads : (part + 1) * quads]
    spread = (
        lax.broadcasted_iota(jnp.int32, (size, pairs), 0) // QUAD
        == lax.broadcasted_iota(jnp.int32, (size, pairs), 1)
    ).astype(jnp.bfloat16)
    tall = jnp.dot(spread, integral_ref[...], preferred_element_type=jnp.float32)
    wide = lax.dot_general(
        tall.astype(jnp.bfloat16),
        spread,
        (((1,), (1,)), ((), ())),
        preferred_element_type=jnp.float32,
    )
    row = lax.broadcasted_iota(jnp.int32, (size, size), 0)
    column = lax.broadcasted_iota(jnp.int32, (size, size), 1)
    kron_ref[...] = jnp.where(row % QUAD == column % QUAD, wide, 0.0).astype(jnp.bfloat16)
    copy.wait()


def prepare(codes, integrals, rows):
    pairs = codes.shape[0]
    size = pairs * QUAD
    return pl.pallas_call(
        prepare_kernel,
        out_shape=[
            jax.ShapeDtypeStruct((size, 128), jnp.int32),
            jax.ShapeDtypeStruct((size, size), jnp.bfloat16),
            jax.ShapeDtypeStruct(rows.shape, rows.dtype),
        ],
        in_specs=[whole(), whole(), any_place()],
        out_specs=[whole(), whole(), any_place()],
        scratch_shapes=[pltpu.SemaphoreType.DMA],
        compiler_params=pltpu.CompilerParams(vmem_limit_bytes=VMEM_LIMIT),
        cost_estimate=pl.CostEstimate(
            flops=0, bytes_accessed=4 * 1024 * 1024, transcendentals=0
        ),
        name="prepare",
    )(codes, integrals, rows)


def pair_images(step, quads, code_ref, kron_ref, turned):
    beta_count, rows = turned.shape
    size = kron_ref.shape[0]
    halves = size // (2 * QUAD)
    own = pltpu.roll(code_ref[...], 128 - step * quads, 1)
    codes = jnp.concatenate(
        [jnp.broadcast_to(own[:, quad : quad + 1], (size, 128)) for quad in range(quads)], axis=0
    )
    target = jnp.right_shift(codes, 2)
    value = ((codes & 3) - 1).astype(jnp.float32)
    lane = lax.broadcasted_iota(jnp.int32, codes.shape, 1)
    onehot = jnp.concatenate(
        [
            jnp.where(lane == target - start, value, 0.0).astype(jnp.bfloat16)
            for start in range(0, beta_count, 128)
        ],
        axis=1,
    )
    coupled = jnp.dot(onehot, turned[...], preferred_element_type=jnp.float32)
    coupled = coupled.astype(jnp.bfloat16)
    low = lax.broadcasted_iota(jnp.int32, (halves, 8, rows), 1) < QUAD
    evens, odds = [], []
    for pair in range(quads // 2):
        first, second = [
            jnp.dot(
                kron_ref[...],
                coupled[at * size : (at + 1) * size],
                preferred_element_type=jnp.float32,
            ).reshape(halves, 8, rows)
            for at in (2 * pair, 2 * pair + 1)
        ]
        evens.append(jnp.where(low, first, pltpu.roll(second, QUAD, 1)))
        odds.append(jnp.where(low, pltpu.roll(first, QUAD, 1), second))
    return [jnp.concatenate(side, axis=1).astype(jnp.bfloat16) for side in (evens, odds)]


def mixed_kernel(count, quads, bundle, place_ref, *refs):
    pieces = refs[:count]
    code_ref, kron_ref, alpha_ref = refs[count : count + 3]
    outs = refs[count + 3 : count + 3 + count // 2]
    rest = refs[count + 3 + count // 2 :]
    held, turned, images, total, lanes, ordered, indices, signs, arrived = rest
    step = pl.program_id(0)
    local_rows = pieces[0].shape[0]
    halves, _, window, block_rows = images.shape
    columns = quads * QUAD

    @pl.when(step == 0)
    def _():
        copies = [
            pltpu.make_async_copy(
                pieces[at], held.at[pl.ds(at * local_rows, local_rows)], arrived.at[at]
            )
            for at in range(count)
        ]
        for copy in copies:
            copy.start()
        for copy in copies:
            copy.wait()
        for start in range(0, block_rows, 128):
            turned[:, start : start + 128] = held[start : start + 128, :].T

    place = pl.ds(pl.multiple_of(step * columns, columns), columns)
    even, odd = pair_images(step, quads, code_ref, kron_ref, turned)
    images[:, 0, place, :] = even
    images[:, 1, place, :] = odd

    @pl.when(step == pl.num_programs(0) - 1)
    def _():
        total[...] = jnp.zeros_like(total)
        indices[...] = jnp.right_shift(alpha_ref[...], 2)
        signs[...] = ((alpha_ref[...] & 3) - 1).astype(jnp.float32)
        position = lax.broadcasted_iota(jnp.int32, (block_rows, block_rows), 0)
        position = jnp.bitwise_xor(position, place_ref[0] * local_rows)

        def body(at, carry):
            term = None
            for offset in range(bundle):
                pair = bundle * at + offset
                selector = jnp.where(
                    position == indices[pl.ds(pair, 1), :], signs[pl.ds(pair, 1), :], 0.0
                ).astype(jnp.bfloat16)
                part = jnp.dot(
                    images[lax.div(pair, 2), lax.rem(pair, 2)],
                    selector,
                    preferred_element_type=jnp.float32,
                )
                term = part if term is None else term + part
            total[...] += term
            return carry

        lax.fori_loop(0, 2 * halves // bundle, body, 0)
        quad_count = window // QUAD
        for at in range(block_rows // 128):
            rows = slice(at * 128, (at + 1) * 128)
            lanes[at] = total[:, rows]
            ordered[rows, :] = jnp.concatenate(
                [lanes[at, pl.ds(part, quad_count, QUAD), :] for part in range(QUAD)], axis=0
            ).T
        for at in range(count):
            start = pl.multiple_of((place_ref[0] ^ at) * local_rows, local_rows)
            rows = slice(at % 2 * local_rows, (at % 2 + 1) * local_rows)
            outs[at // 2][rows, :] = ordered[pl.ds(start, local_rows), :]


def mixed_pieces(place, pieces, codes, kron, alpha_codes, window):
    count = len(pieces)
    local_rows, beta_count = pieces[0].shape
    pairs, block_rows = alpha_codes.shape
    columns = min(128, window, 128 * 512 // block_rows)
    bundle = next(size for size in (25, 10, 5, 2, 1) if pairs % size == 0)
    flops = 2 * window * pairs * block_rows * (beta_count + pairs * QUAD + block_rows)
    return pl.pallas_call(
        functools.partial(mixed_kernel, count, columns // QUAD, bundle),
        out_shape=[jax.ShapeDtypeStruct((2 * local_rows, window), jnp.float32)] * (count // 2),
        grid_spec=pltpu.PrefetchScalarGridSpec(
            num_scalar_prefetch=1,
            grid=(window // columns,),
            in_specs=[any_place()] * count
            + [whole()] * 3,
            out_specs=[whole()] * (count // 2),
            scratch_shapes=[
                pltpu.VMEM((block_rows, beta_count), jnp.bfloat16),
                pltpu.VMEM((beta_count, block_rows), jnp.bfloat16),
                pltpu.VMEM((pairs // 2, 2, window, block_rows), jnp.bfloat16),
                pltpu.VMEM((window, block_rows), jnp.float32),
                pltpu.VMEM((block_rows // 128, window, 128), jnp.float32),
                pltpu.VMEM((block_rows, window), jnp.float32),
                pltpu.VMEM((pairs, block_rows), jnp.int32),
                pltpu.VMEM((pairs, block_rows), jnp.float32),
                pltpu.SemaphoreType.DMA((count,)),
            ],
        ),
        compiler_params=pltpu.CompilerParams(
            dimension_semantics=("arbitrary",), vmem_limit_bytes=VMEM_LIMIT
        ),
        cost_estimate=pl.CostEstimate(flops=flops, bytes_accessed=1 << 20, transcendentals=0),
        name="mixed",
    )(place, *pieces, codes, kron, alpha_codes)


def plain_kernel(count, place_ref, *refs):
    pieces = refs[:count]
    alpha_source, beta_source, out_ref, block, alpha_ref, beta_ref, arrived = refs[count:]
    local_rows = pieces[0].shape[0]
    copies = [
        pltpu.make_async_copy(alpha_source, alpha_ref, arrived.at[count]),
        pltpu.make_async_copy(beta_source, beta_ref, arrived.at[count + 1]),
    ]
    for at in range(count):
        start = pl.multiple_of((place_ref[0] ^ at) * local_rows, local_rows)
        copies.append(
            pltpu.make_async_copy(
                pieces[at], block.at[pl.ds(start, local_rows)], arrived.at[at]
            )
        )
    for copy in copies:
        copy.start()
    for copy in copies:
        copy.wait()
    start = pl.multiple_of(place_ref[0] * local_rows, local_rows)
    out_ref[...] = jnp.dot(
        alpha_ref[...], block[...], preferred_element_type=jnp.float32
    ) + jnp.dot(
        block[pl.ds(start, local_rows), :], beta_ref[...], preferred_element_type=jnp.float32
    )


def plain_terms(place, pieces, alpha_operator, beta_operator):
    count = len(pieces)
    local_rows, beta_count = pieces[0].shape
    block_rows = alpha_operator.shape[1]
    return pl.pallas_call(
        functools.partial(plain_kernel, count),
        out_shape=jax.ShapeDtypeStruct((local_rows, beta_count), jnp.float32),
        in_specs=[pl.BlockSpec(memory_space=pltpu.SMEM)]
        + [any_place()] * count
        + [in_hbm(), in_hbm()],
        out_specs=whole(),
        scratch_shapes=[
            pltpu.VMEM((block_rows, beta_count), jnp.bfloat16),
            pltpu.VMEM(alpha_operator.shape, jnp.bfloat16),
            pltpu.VMEM(beta_operator.shape, jnp.bfloat16),
            pltpu.SemaphoreType.DMA((count + 2,)),
        ],
        compiler_params=pltpu.CompilerParams(vmem_limit_bytes=VMEM_LIMIT),
        cost_estimate=pl.CostEstimate(
            flops=2 * local_rows * beta_count * (beta_count + block_rows),
            bytes_accessed=2 * beta_count * (beta_count + block_rows),
            transcendentals=0,
        ),
        name="plain",
    )(place, *pieces, alpha_operator, beta_operator)


def add_kernel(count, classes, place_ref, base_ref, *refs):
    own, passed = refs[:count], refs[count : 2 * count]
    out_ref, held, arrived = refs[2 * count :]
    local_rows, window = held.shape[1:]
    copies = []
    for at in range(count):
        for side, source in enumerate((own[at], passed[at])):
            slot = 2 * at + side
            rows = source.at[pl.ds(side * local_rows, local_rows)]
            copies.append(pltpu.make_async_copy(rows, held.at[slot], arrived.at[slot]))
    for copy in copies:
        copy.start()
    chunk = place_ref[0] // classes
    for at in range(count):
        copies[2 * at].wait()
        copies[2 * at + 1].wait()
        columns = pl.ds(pl.multiple_of((chunk ^ at) * window, window), window)
        out_ref[:, columns] = base_ref[:, columns] + (held[2 * at] + held[2 * at + 1])


def add_terms(place, base, own, passed, classes):
    count = len(own)
    rows, window = own[0].shape
    return pl.pallas_call(
        functools.partial(add_kernel, count, classes),
        out_shape=jax.ShapeDtypeStruct(base.shape, jnp.float32),
        in_specs=[pl.BlockSpec(memory_space=pltpu.SMEM), whole()] + [any_place()] * (2 * count),
        out_specs=whole(),
        scratch_shapes=[
            pltpu.VMEM((2 * count, rows // 2, window), jnp.float32),
            pltpu.SemaphoreType.DMA((2 * count,)),
        ],
        compiler_params=pltpu.CompilerParams(vmem_limit_bytes=VMEM_LIMIT),
        name="add",
    )(place, base, *own, *passed)


def local(
    civec, beta_index, beta_sign, alpha_index, alpha_sign, integrals, beta_operator, alpha_operator
):
    classes, pair_count = integrals.shape[:2]
    local_rows, beta_count = civec.shape
    count = lax.axis_size("str")
    blocks = lax.axis_size("blk")
    block_rows = local_rows * count
    window = beta_count * classes // count
    block_at, place = lax.axis_index("blk"), lax.axis_index("str")
    symmetry = place % classes
    partner = jnp.bitwise_xor(block_at, 1 << symmetry)

    def near(array, distance):
        route = [
            (blk * count + at, blk * count + (at ^ distance))
            for blk in range(blocks)
            for at in range(count)
        ]
        return lax.ppermute(array, ("blk", "str"), route)

    def far(array, distance):
        route = [
            (blk * count + at, (blk ^ (1 << at % classes)) * count + (at ^ distance))
            for blk in range(blocks)
            for at in range(count)
        ]
        return lax.ppermute(array, ("blk", "str"), route)

    def one_class(array, start, width):
        return lax.dynamic_slice(array, (symmetry, 0, start), (1, array.shape[1], width))[0]

    def row_codes(index, sign, start, width):
        return one_class(index, start, width) * 4 + one_class(sign, start, width) + 1

    beta_codes = row_codes(beta_index, beta_sign, place // classes * window, window)
    alpha_codes = row_codes(alpha_index, alpha_sign, partner * block_rows, block_rows)
    own_integrals = one_class(integrals, 0, pair_count)
    arrived = [near(civec, at) for at in range(2, count, 2)]
    place = place.astype(jnp.int32).reshape(1)
    codes, kron, rows = prepare(beta_codes, own_integrals, civec)
    codes, alpha_codes, *arrived = lax.optimization_barrier((codes, alpha_codes, *arrived))
    straight = [rows] + arrived
    crossed = [near(piece, 1) for piece in [civec] + arrived]
    pieces = [piece for two in zip(straight, crossed) for piece in two]

    sent = mixed_pieces(place, pieces, codes, kron, alpha_codes, window)
    own = [far(sent[at], 2 * at) for at in range(count // 2)]
    base = plain_terms(place, pieces, alpha_operator, beta_operator)
    own[-1], base = lax.optimization_barrier((own[-1], base))
    passed = [near(rows, 1) for rows in own]
    return add_terms(place, base, own, passed, classes)


def solution(mesh):
    placed = (P(("blk", "str"), None), P(), P(), P(), P(), P(), P(), P(("blk", "str"), None))
    return jax.shard_map(
        local, mesh=mesh, in_specs=placed, out_specs=P(("blk", "str"), None), check_vma=False
    )
```

```python
import functools

import jax
import jax.numpy as jnp
from jax import lax
from jax.experimental import pallas as pl
from jax.experimental.pallas import tpu as pltpu
from jax.sharding import PartitionSpec as P

QUAD = 4
VMEM_LIMIT = 46 * 1024 * 1024


def whole():
    return pl.BlockSpec(memory_space=pltpu.VMEM)


def any_place():
    return pl.BlockSpec(memory_space=pl.ANY)


def in_hbm():
    return pl.BlockSpec(memory_space=pltpu.HBM)


def prepare_kernel(code_ref, integral_ref, rows_ref, out_ref, kron_ref, copied_ref, arrived):
    pairs, window = code_ref.shape
    quads = window // QUAD
    size = pairs * QUAD
    copy = pltpu.make_async_copy(rows_ref, copied_ref, arrived)
    copy.start()
    codes = code_ref[...]
    for part in range(QUAD):
        out_ref[pl.ds(part, pairs, QUAD), :quads] = codes[:, part * quads : (part + 1) * quads]
    spread = (
        lax.broadcasted_iota(jnp.int32, (size, pairs), 0) // QUAD
        == lax.broadcasted_iota(jnp.int32, (size, pairs), 1)
    ).astype(jnp.bfloat16)
    tall = jnp.dot(spread, integral_ref[...], preferred_element_type=jnp.float32)
    wide = lax.dot_general(
        tall.astype(jnp.bfloat16),
        spread,
        (((1,), (1,)), ((), ())),
        preferred_element_type=jnp.float32,
    )
    row = lax.broadcasted_iota(jnp.int32, (size, size), 0)
    column = lax.broadcasted_iota(jnp.int32, (size, size), 1)
    kron_ref[...] = jnp.where(row % QUAD == column % QUAD, wide, 0.0).astype(jnp.bfloat16)
    copy.wait()


def prepare(codes, integrals, rows):
    pairs = codes.shape[0]
    size = pairs * QUAD
    return pl.pallas_call(
        prepare_kernel,
        out_shape=[
            jax.ShapeDtypeStruct((size, 128), jnp.int32),
            jax.ShapeDtypeStruct((size, size), jnp.bfloat16),
            jax.ShapeDtypeStruct(rows.shape, rows.dtype),
        ],
        in_specs=[whole(), whole(), any_place()],
        out_specs=[whole(), whole(), any_place()],
        scratch_shapes=[pltpu.SemaphoreType.DMA],
        compiler_params=pltpu.CompilerParams(vmem_limit_bytes=VMEM_LIMIT),
        cost_estimate=pl.CostEstimate(
            flops=0, bytes_accessed=4 * 1024 * 1024, transcendentals=0
        ),
        name="prepare",
    )(codes, integrals, rows)


def pair_images(step, quads, code_ref, kron_ref, turned):
    beta_count, rows = turned.shape
    size = kron_ref.shape[0]
    halves = size // (2 * QUAD)
    own = pltpu.roll(code_ref[...], 128 - step * quads, 1)
    codes = jnp.concatenate(
        [jnp.broadcast_to(own[:, quad : quad + 1], (size, 128)) for quad in range(quads)], axis=0
    )
    target = jnp.right_shift(codes, 2).astype(jnp.int16)
    value = ((codes & 3) - 1).astype(jnp.float32).astype(jnp.bfloat16)
    lane = lax.broadcasted_iota(jnp.int32, codes.shape, 1).astype(jnp.int16)
    onehot = jnp.concatenate(
        [
            jnp.where(lane == target - jnp.int16(start), value, jnp.zeros((), jnp.bfloat16))
            for start in range(0, beta_count, 128)
        ],
        axis=1,
    )
    coupled = jnp.dot(onehot, turned[...], preferred_element_type=jnp.float32)
    coupled = coupled.astype(jnp.bfloat16)
    low = lax.broadcasted_iota(jnp.int32, (halves, 8, rows), 1) < QUAD
    evens, odds = [], []
    for pair in range(quads // 2):
        first, second = [
            jnp.dot(
                kron_ref[...],
                coupled[at * size : (at + 1) * size],
                preferred_element_type=jnp.float32,
            ).reshape(halves, 8, rows)
            for at in (2 * pair, 2 * pair + 1)
        ]
        evens.append(jnp.where(low, first, pltpu.roll(second, QUAD, 1)))
        odds.append(jnp.where(low, pltpu.roll(first, QUAD, 1), second))
    return [jnp.concatenate(side, axis=1).astype(jnp.bfloat16) for side in (evens, odds)]


def mixed_kernel(count, quads, bundle, place_ref, *refs):
    pieces = refs[:count]
    code_ref, kron_ref, alpha_ref = refs[count : count + 3]
    outs = refs[count + 3 : count + 3 + count // 2]
    rest = refs[count + 3 + count // 2 :]
    held, turned, images, total, lanes, ordered, indices, signs, arrived = rest
    step = pl.program_id(0)
    local_rows = pieces[0].shape[0]
    halves, _, window, block_rows = images.shape
    columns = quads * QUAD

    @pl.when(step == 0)
    def _():
        copies = [
            pltpu.make_async_copy(
                pieces[at], held.at[pl.ds(at * local_rows, local_rows)], arrived.at[at]
            )
            for at in range(count)
        ]
        for copy in copies:
            copy.start()
        for copy in copies:
            copy.wait()
        for start in range(0, block_rows, 128):
            turned[:, start : start + 128] = held[start : start + 128, :].T

    place = pl.ds(pl.multiple_of(step * columns, columns), columns)
    even, odd = pair_images(step, quads, code_ref, kron_ref, turned)
    images[:, 0, place, :] = even
    images[:, 1, place, :] = odd

    @pl.when(step == pl.num_programs(0) - 1)
    def _():
        total[...] = jnp.zeros_like(total)
        indices[...] = jnp.right_shift(alpha_ref[...], 2)
        signs[...] = ((alpha_ref[...] & 3) - 1).astype(jnp.float32)
        position = lax.broadcasted_iota(jnp.int32, (block_rows, block_rows), 0)
        position = jnp.bitwise_xor(position, place_ref[0] * local_rows)

        def body(at, carry):
            term = None
            for offset in range(bundle):
                pair = bundle * at + offset
                selector = jnp.where(
                    position == indices[pl.ds(pair, 1), :], signs[pl.ds(pair, 1), :], 0.0
                ).astype(jnp.bfloat16)
                part = jnp.dot(
                    images[lax.div(pair, 2), lax.rem(pair, 2)],
                    selector,
                    preferred_element_type=jnp.float32,
                )
                term = part if term is None else term + part
            total[...] += term
            return carry

        lax.fori_loop(0, 2 * halves // bundle, body, 0)
        quad_count = window // QUAD
        for at in range(block_rows // 128):
            rows = slice(at * 128, (at + 1) * 128)
            lanes[at] = total[:, rows]
            ordered[rows, :] = jnp.concatenate(
                [lanes[at, pl.ds(part, quad_count, QUAD), :] for part in range(QUAD)], axis=0
            ).T
        for at in range(count):
            start = pl.multiple_of((place_ref[0] ^ at) * local_rows, local_rows)
            rows = slice(at % 2 * local_rows, (at % 2 + 1) * local_rows)
            outs[at // 2][rows, :] = ordered[pl.ds(start, local_rows), :]


def mixed_pieces(place, pieces, codes, kron, alpha_codes, window):
    count = len(pieces)
    local_rows, beta_count = pieces[0].shape
    pairs, block_rows = alpha_codes.shape
    columns = min(128, window, 128 * 512 // block_rows)
    bundle = next(size for size in (25, 10, 5, 2, 1) if pairs % size == 0)
    flops = 2 * window * pairs * block_rows * (beta_count + pairs * QUAD + block_rows)
    return pl.pallas_call(
        functools.partial(mixed_kernel, count, columns // QUAD, bundle),
        out_shape=[jax.ShapeDtypeStruct((2 * local_rows, window), jnp.float32)] * (count // 2),
        grid_spec=pltpu.PrefetchScalarGridSpec(
            num_scalar_prefetch=1,
            grid=(window // columns,),
            in_specs=[any_place()] * count
            + [whole()] * 3,
            out_specs=[whole()] * (count // 2),
            scratch_shapes=[
                pltpu.VMEM((block_rows, beta_count), jnp.bfloat16),
                pltpu.VMEM((beta_count, block_rows), jnp.bfloat16),
                pltpu.VMEM((pairs // 2, 2, window, block_rows), jnp.bfloat16),
                pltpu.VMEM((window, block_rows), jnp.float32),
                pltpu.VMEM((block_rows // 128, window, 128), jnp.float32),
                pltpu.VMEM((block_rows, window), jnp.float32),
                pltpu.VMEM((pairs, block_rows), jnp.int32),
                pltpu.VMEM((pairs, block_rows), jnp.float32),
                pltpu.SemaphoreType.DMA((count,)),
            ],
        ),
        compiler_params=pltpu.CompilerParams(
            dimension_semantics=("arbitrary",), vmem_limit_bytes=VMEM_LIMIT
        ),
        cost_estimate=pl.CostEstimate(flops=flops, bytes_accessed=1 << 20, transcendentals=0),
        name="mixed",
    )(place, *pieces, codes, kron, alpha_codes)


def plain_kernel(count, place_ref, *refs):
    pieces = refs[:count]
    alpha_source, beta_source, out_ref, block, alpha_ref, beta_ref, arrived = refs[count:]
    local_rows = pieces[0].shape[0]
    copies = [
        pltpu.make_async_copy(alpha_source, alpha_ref, arrived.at[count]),
        pltpu.make_async_copy(beta_source, beta_ref, arrived.at[count + 1]),
    ]
    for at in range(count):
        start = pl.multiple_of((place_ref[0] ^ at) * local_rows, local_rows)
        copies.append(
            pltpu.make_async_copy(
                pieces[at], block.at[pl.ds(start, local_rows)], arrived.at[at]
            )
        )
    for copy in copies:
        copy.start()
    for copy in copies:
        copy.wait()
    start = pl.multiple_of(place_ref[0] * local_rows, local_rows)
    out_ref[...] = jnp.dot(
        alpha_ref[...], block[...], preferred_element_type=jnp.float32
    ) + jnp.dot(
        block[pl.ds(start, local_rows), :], beta_ref[...], preferred_element_type=jnp.float32
    )


def plain_terms(place, pieces, alpha_operator, beta_operator):
    count = len(pieces)
    local_rows, beta_count = pieces[0].shape
    block_rows = alpha_operator.shape[1]
    return pl.pallas_call(
        functools.partial(plain_kernel, count),
        out_shape=jax.ShapeDtypeStruct((local_rows, beta_count), jnp.float32),
        in_specs=[pl.BlockSpec(memory_space=pltpu.SMEM)]
        + [any_place()] * count
        + [in_hbm(), in_hbm()],
        out_specs=whole(),
        scratch_shapes=[
            pltpu.VMEM((block_rows, beta_count), jnp.bfloat16),
            pltpu.VMEM(alpha_operator.shape, jnp.bfloat16),
            pltpu.VMEM(beta_operator.shape, jnp.bfloat16),
            pltpu.SemaphoreType.DMA((count + 2,)),
        ],
        compiler_params=pltpu.CompilerParams(vmem_limit_bytes=VMEM_LIMIT),
        cost_estimate=pl.CostEstimate(
            flops=2 * local_rows * beta_count * (beta_count + block_rows),
            bytes_accessed=2 * beta_count * (beta_count + block_rows),
            transcendentals=0,
        ),
        name="plain",
    )(place, *pieces, alpha_operator, beta_operator)


def add_kernel(count, classes, place_ref, base_ref, *refs):
    own, passed = refs[:count], refs[count : 2 * count]
    out_ref, held, arrived = refs[2 * count :]
    local_rows, window = held.shape[1:]
    copies = []
    for at in range(count):
        for side, source in enumerate((own[at], passed[at])):
            slot = 2 * at + side
            rows = source.at[pl.ds(side * local_rows, local_rows)]
            copies.append(pltpu.make_async_copy(rows, held.at[slot], arrived.at[slot]))
    for copy in copies:
        copy.start()
    chunk = place_ref[0] // classes
    for at in range(count):
        copies[2 * at].wait()
        copies[2 * at + 1].wait()
        columns = pl.ds(pl.multiple_of((chunk ^ at) * window, window), window)
        out_ref[:, columns] = base_ref[:, columns] + (held[2 * at] + held[2 * at + 1])


def add_terms(place, base, own, passed, classes):
    count = len(own)
    rows, window = own[0].shape
    return pl.pallas_call(
        functools.partial(add_kernel, count, classes),
        out_shape=jax.ShapeDtypeStruct(base.shape, jnp.float32),
        in_specs=[pl.BlockSpec(memory_space=pltpu.SMEM), whole()] + [any_place()] * (2 * count),
        out_specs=whole(),
        scratch_shapes=[
            pltpu.VMEM((2 * count, rows // 2, window), jnp.float32),
            pltpu.SemaphoreType.DMA((2 * count,)),
        ],
        compiler_params=pltpu.CompilerParams(vmem_limit_bytes=VMEM_LIMIT),
        name="add",
    )(place, base, *own, *passed)


def local(
    civec, beta_index, beta_sign, alpha_index, alpha_sign, integrals, beta_operator, alpha_operator
):
    classes, pair_count = integrals.shape[:2]
    local_rows, beta_count = civec.shape
    count = lax.axis_size("str")
    blocks = lax.axis_size("blk")
    block_rows = local_rows * count
    window = beta_count * classes // count
    block_at, place = lax.axis_index("blk"), lax.axis_index("str")
    symmetry = place % classes
    partner = jnp.bitwise_xor(block_at, 1 << symmetry)

    def near(array, distance):
        route = [
            (blk * count + at, blk * count + (at ^ distance))
            for blk in range(blocks)
            for at in range(count)
        ]
        return lax.ppermute(array, ("blk", "str"), route)

    def far(array, distance):
        route = [
            (blk * count + at, (blk ^ (1 << at % classes)) * count + (at ^ distance))
            for blk in range(blocks)
            for at in range(count)
        ]
        return lax.ppermute(array, ("blk", "str"), route)

    def one_class(array, start, width):
        return lax.dynamic_slice(array, (symmetry, 0, start), (1, array.shape[1], width))[0]

    def row_codes(index, sign, start, width):
        return one_class(index, start, width) * 4 + one_class(sign, start, width) + 1

    beta_codes = row_codes(beta_index, beta_sign, place // classes * window, window)
    alpha_codes = row_codes(alpha_index, alpha_sign, partner * block_rows, block_rows)
    own_integrals = one_class(integrals, 0, pair_count)
    place = place.astype(jnp.int32).reshape(1)
    codes, kron, rows = prepare(beta_codes, own_integrals, civec)
    later, place = lax.optimization_barrier((civec, place))
    arrived = [near(later if at == 2 else civec, at) for at in range(2, count, 2)]
    codes, alpha_codes, arrived[0] = lax.optimization_barrier((codes, alpha_codes, arrived[0]))
    crossed = [near(piece, 1) for piece in [civec] + arrived]
    pieces = [piece for two in zip([rows] + arrived, crossed) for piece in two]

    sent = mixed_pieces(place, pieces, codes, kron, alpha_codes, window)
    own = [far(sent[at], 2 * at) for at in reversed(range(count // 2))][::-1]
    base = plain_terms(place, pieces, alpha_operator, beta_operator)
    own[0], base = lax.optimization_barrier((own[0], base))
    passed = [near(rows, 1) for rows in own]
    return add_terms(place, base, own, passed, classes)


def solution(mesh):
    placed = (P(("blk", "str"), None), P(), P(), P(), P(), P(), P(), P(("blk", "str"), None))
    return jax.shard_map(
        local, mesh=mesh, in_specs=placed, out_specs=P(("blk", "str"), None), check_vma=False
    )
```

```python
import functools

import jax
import jax.numpy as jnp
from jax import lax
from jax.experimental import pallas as pl
from jax.experimental.pallas import tpu as pltpu
from jax.sharding import PartitionSpec as P

QUAD = 4
SPAN = 120.0
SMALLEST = 2.0**-100
SCALE_ROWS = 16
VMEM_LIMIT = 46 * 1024 * 1024


def whole():
    return pl.BlockSpec(memory_space=pltpu.VMEM)


def coded(values):
    largest = jnp.max(jnp.abs(values), axis=(0, 1), keepdims=True)
    scale = (jnp.maximum(largest, SMALLEST) * 1.01).astype(jnp.bfloat16)
    share = jnp.sqrt(jnp.abs(values) * (1.0 / scale.astype(jnp.float32)))
    size = jnp.exp2((share * 2.0 - 1.0) * SPAN)
    return jnp.where(values < 0.0, -size, size).astype(jnp.bfloat16), scale


def decoded(codes, scale):
    codes, scale = codes.astype(jnp.float32), scale.astype(jnp.float32)
    share = jnp.log2(jnp.abs(codes)) * (0.5 / SPAN) + 0.5
    value = share * share * scale
    return jnp.where(codes < 0.0, -value, value)


def any_place():
    return pl.BlockSpec(memory_space=pl.ANY)


def in_hbm():
    return pl.BlockSpec(memory_space=pltpu.HBM)


def prepare_kernel(code_ref, integral_ref, rows_ref, out_ref, kron_ref, copied_ref, arrived):
    pairs, window = code_ref.shape
    quads = window // QUAD
    size = pairs * QUAD
    copy = pltpu.make_async_copy(rows_ref, copied_ref, arrived)
    copy.start()
    codes = code_ref[...]
    for part in range(QUAD):
        out_ref[pl.ds(part, pairs, QUAD), :quads] = codes[:, part * quads : (part + 1) * quads]
    spread = (
        lax.broadcasted_iota(jnp.int32, (size, pairs), 0) // QUAD
        == lax.broadcasted_iota(jnp.int32, (size, pairs), 1)
    ).astype(jnp.bfloat16)
    tall = jnp.dot(spread, integral_ref[...], preferred_element_type=jnp.float32)
    wide = lax.dot_general(
        tall.astype(jnp.bfloat16),
        spread,
        (((1,), (1,)), ((), ())),
        preferred_element_type=jnp.float32,
    )
    row = lax.broadcasted_iota(jnp.int32, (size, size), 0)
    column = lax.broadcasted_iota(jnp.int32, (size, size), 1)
    kron_ref[...] = jnp.where(row % QUAD == column % QUAD, wide, 0.0).astype(jnp.bfloat16)
    copy.wait()


def prepare(codes, integrals, rows):
    pairs = codes.shape[0]
    size = pairs * QUAD
    return pl.pallas_call(
        prepare_kernel,
        out_shape=[
            jax.ShapeDtypeStruct((size, 128), jnp.int32),
            jax.ShapeDtypeStruct((size, size), jnp.bfloat16),
            jax.ShapeDtypeStruct(rows.shape, rows.dtype),
        ],
        in_specs=[whole(), whole(), any_place()],
        out_specs=[whole(), whole(), any_place()],
        scratch_shapes=[pltpu.SemaphoreType.DMA],
        compiler_params=pltpu.CompilerParams(vmem_limit_bytes=VMEM_LIMIT),
        cost_estimate=pl.CostEstimate(
            flops=0, bytes_accessed=4 * 1024 * 1024, transcendentals=0
        ),
        name="prepare",
    )(codes, integrals, rows)


def pair_images(step, quads, code_ref, kron_ref, turned):
    beta_count, rows = turned.shape
    size = kron_ref.shape[0]
    halves = size // (2 * QUAD)
    own = pltpu.roll(code_ref[...], 128 - step * quads, 1)
    codes = jnp.concatenate(
        [jnp.broadcast_to(own[:, quad : quad + 1], (size, 128)) for quad in range(quads)], axis=0
    )
    target = jnp.right_shift(codes, 2).astype(jnp.int16)
    value = ((codes & 3) - 1).astype(jnp.float32).astype(jnp.bfloat16)
    lane = lax.broadcasted_iota(jnp.int32, codes.shape, 1).astype(jnp.int16)
    onehot = jnp.concatenate(
        [
            jnp.where(lane == target - jnp.int16(start), value, jnp.zeros((), jnp.bfloat16))
            for start in range(0, beta_count, 128)
        ],
        axis=1,
    )
    coupled = jnp.dot(onehot, turned[...], preferred_element_type=jnp.float32)
    coupled = coupled.astype(jnp.bfloat16)
    low = lax.broadcasted_iota(jnp.int32, (halves, 8, rows), 1) < QUAD
    evens, odds = [], []
    for pair in range(quads // 2):
        first, second = [
            jnp.dot(
                kron_ref[...],
                coupled[at * size : (at + 1) * size],
                preferred_element_type=jnp.float32,
            ).reshape(halves, 8, rows)
            for at in (2 * pair, 2 * pair + 1)
        ]
        evens.append(jnp.where(low, first, pltpu.roll(second, QUAD, 1)))
        odds.append(jnp.where(low, pltpu.roll(first, QUAD, 1), second))
    return [jnp.concatenate(side, axis=1).astype(jnp.bfloat16) for side in (evens, odds)]


def mixed_kernel(count, quads, bundle, place_ref, *refs):
    pieces = refs[:count]
    code_ref, kron_ref, alpha_ref = refs[count : count + 3]
    outs = refs[count + 3 : count + 3 + count // 2]
    rest = refs[count + 3 + count // 2 :]
    held, turned, images, total, lanes, ordered, indices, signs, arrived = rest
    step = pl.program_id(0)
    local_rows = pieces[0].shape[0]
    halves, _, window, block_rows = images.shape
    columns = quads * QUAD

    @pl.when(step == 0)
    def _():
        copies = [
            pltpu.make_async_copy(
                pieces[at], held.at[pl.ds(at * local_rows, local_rows)], arrived.at[at]
            )
            for at in range(count)
        ]
        for copy in copies:
            copy.start()
        for copy in copies:
            copy.wait()
        for start in range(0, block_rows, 128):
            turned[:, start : start + 128] = held[start : start + 128, :].T

    place = pl.ds(pl.multiple_of(step * columns, columns), columns)
    even, odd = pair_images(step, quads, code_ref, kron_ref, turned)
    images[:, 0, place, :] = even
    images[:, 1, place, :] = odd

    @pl.when(step == pl.num_programs(0) - 1)
    def _():
        total[...] = jnp.zeros_like(total)
        indices[...] = jnp.right_shift(alpha_ref[...], 2)
        signs[...] = ((alpha_ref[...] & 3) - 1).astype(jnp.float32)
        position = lax.broadcasted_iota(jnp.int32, (block_rows, block_rows), 0)
        position = jnp.bitwise_xor(position, place_ref[0] * local_rows)

        def body(at, carry):
            term = None
            for offset in range(bundle):
                pair = bundle * at + offset
                selector = jnp.where(
                    position == indices[pl.ds(pair, 1), :], signs[pl.ds(pair, 1), :], 0.0
                ).astype(jnp.bfloat16)
                part = jnp.dot(
                    images[lax.div(pair, 2), lax.rem(pair, 2)],
                    selector,
                    preferred_element_type=jnp.float32,
                )
                term = part if term is None else term + part
            total[...] += term
            return carry

        lax.fori_loop(0, 2 * halves // bundle, body, 0)
        quad_count = window // QUAD
        codes, scale = coded(total[...])
        total[...] = codes.astype(jnp.float32)
        for at in range(block_rows // 128):
            rows = slice(at * 128, (at + 1) * 128)
            lanes[at] = total[:, rows]
            ordered[rows, :] = jnp.concatenate(
                [lanes[at, pl.ds(part, quad_count, QUAD), :] for part in range(QUAD)], axis=0
            ).T.astype(jnp.bfloat16)
        for at in range(count // 2):
            outs[at][2 * local_rows :, :] = jnp.broadcast_to(scale, (SCALE_ROWS, window))
        for at in range(count):
            start = pl.multiple_of((place_ref[0] ^ at) * local_rows, local_rows)
            rows = slice(at % 2 * local_rows, (at % 2 + 1) * local_rows)
            outs[at // 2][rows, :] = ordered[pl.ds(start, local_rows), :]


def mixed_pieces(place, pieces, codes, kron, alpha_codes, window):
    count = len(pieces)
    local_rows, beta_count = pieces[0].shape
    pairs, block_rows = alpha_codes.shape
    columns = min(128, window, 128 * 512 // block_rows)
    bundle = next(size for size in (25, 10, 5, 2, 1) if pairs % size == 0)
    flops = 2 * window * pairs * block_rows * (beta_count + pairs * QUAD + block_rows)
    return pl.pallas_call(
        functools.partial(mixed_kernel, count, columns // QUAD, bundle),
        out_shape=[jax.ShapeDtypeStruct((2 * local_rows + SCALE_ROWS, window), jnp.bfloat16)]
        * (count // 2),
        grid_spec=pltpu.PrefetchScalarGridSpec(
            num_scalar_prefetch=1,
            grid=(window // columns,),
            in_specs=[any_place()] * count
            + [whole()] * 3,
            out_specs=[whole()] * (count // 2),
            scratch_shapes=[
                pltpu.VMEM((block_rows, beta_count), jnp.bfloat16),
                pltpu.VMEM((beta_count, block_rows), jnp.bfloat16),
                pltpu.VMEM((pairs // 2, 2, window, block_rows), jnp.bfloat16),
                pltpu.VMEM((window, block_rows), jnp.float32),
                pltpu.VMEM((block_rows // 128, window, 128), jnp.float32),
                pltpu.VMEM((block_rows, window), jnp.bfloat16),
                pltpu.VMEM((pairs, block_rows), jnp.int32),
                pltpu.VMEM((pairs, block_rows), jnp.float32),
                pltpu.SemaphoreType.DMA((count,)),
            ],
        ),
        compiler_params=pltpu.CompilerParams(
            dimension_semantics=("arbitrary",), vmem_limit_bytes=VMEM_LIMIT
        ),
        cost_estimate=pl.CostEstimate(flops=flops, bytes_accessed=1 << 20, transcendentals=0),
        name="mixed",
    )(place, *pieces, codes, kron, alpha_codes)


def plain_kernel(count, place_ref, *refs):
    pieces = refs[:count]
    alpha_source, beta_source, out_ref, block, alpha_ref, beta_ref, arrived = refs[count:]
    local_rows = pieces[0].shape[0]
    copies = [
        pltpu.make_async_copy(alpha_source, alpha_ref, arrived.at[count]),
        pltpu.make_async_copy(beta_source, beta_ref, arrived.at[count + 1]),
    ]
    for at in range(count):
        start = pl.multiple_of((place_ref[0] ^ at) * local_rows, local_rows)
        copies.append(
            pltpu.make_async_copy(
                pieces[at], block.at[pl.ds(start, local_rows)], arrived.at[at]
            )
        )
    for copy in copies:
        copy.start()
    for copy in copies:
        copy.wait()
    start = pl.multiple_of(place_ref[0] * local_rows, local_rows)
    out_ref[...] = jnp.dot(
        alpha_ref[...], block[...], preferred_element_type=jnp.float32
    ) + jnp.dot(
        block[pl.ds(start, local_rows), :], beta_ref[...], preferred_element_type=jnp.float32
    )


def plain_terms(place, pieces, alpha_operator, beta_operator):
    count = len(pieces)
    local_rows, beta_count = pieces[0].shape
    block_rows = alpha_operator.shape[1]
    return pl.pallas_call(
        functools.partial(plain_kernel, count),
        out_shape=jax.ShapeDtypeStruct((local_rows, beta_count), jnp.float32),
        in_specs=[pl.BlockSpec(memory_space=pltpu.SMEM)]
        + [any_place()] * count
        + [in_hbm(), in_hbm()],
        out_specs=whole(),
        scratch_shapes=[
            pltpu.VMEM((block_rows, beta_count), jnp.bfloat16),
            pltpu.VMEM(alpha_operator.shape, jnp.bfloat16),
            pltpu.VMEM(beta_operator.shape, jnp.bfloat16),
            pltpu.SemaphoreType.DMA((count + 2,)),
        ],
        compiler_params=pltpu.CompilerParams(vmem_limit_bytes=VMEM_LIMIT),
        cost_estimate=pl.CostEstimate(
            flops=2 * local_rows * beta_count * (beta_count + block_rows),
            bytes_accessed=2 * beta_count * (beta_count + block_rows),
            transcendentals=0,
        ),
        name="plain",
    )(place, *pieces, alpha_operator, beta_operator)


def add_kernel(count, classes, place_ref, base_ref, *refs):
    own, passed = refs[:count], refs[count : 2 * count]
    out_ref, held, scales, arrived = refs[2 * count :]
    local_rows, window = held.shape[1:]
    copies = []
    for at in range(count):
        for side, source in enumerate((own[at], passed[at])):
            slot = 2 * at + side
            rows = source.at[pl.ds(side * local_rows, local_rows)]
            scale = source.at[pl.ds(2 * local_rows, SCALE_ROWS)]
            copies.append(pltpu.make_async_copy(rows, held.at[slot], arrived.at[slot, 0]))
            copies.append(pltpu.make_async_copy(scale, scales.at[slot], arrived.at[slot, 1]))
    for copy in copies:
        copy.start()
    chunk = place_ref[0] // classes
    for at in range(count):
        for copy in copies[4 * at : 4 * at + 4]:
            copy.wait()
        columns = pl.ds(pl.multiple_of((chunk ^ at) * window, window), window)
        out_ref[:, columns] = base_ref[:, columns] + (
            decoded(held[2 * at], scales[2 * at, :1, :1])
            + decoded(held[2 * at + 1], scales[2 * at + 1, :1, :1])
        )


def add_terms(place, base, own, passed, classes):
    count = len(own)
    rows, window = own[0].shape
    local_rows = (rows - SCALE_ROWS) // 2
    return pl.pallas_call(
        functools.partial(add_kernel, count, classes),
        out_shape=jax.ShapeDtypeStruct(base.shape, jnp.float32),
        in_specs=[pl.BlockSpec(memory_space=pltpu.SMEM), whole()] + [any_place()] * (2 * count),
        out_specs=whole(),
        scratch_shapes=[
            pltpu.VMEM((2 * count, local_rows, window), jnp.bfloat16),
            pltpu.VMEM((2 * count, SCALE_ROWS, window), jnp.bfloat16),
            pltpu.SemaphoreType.DMA((2 * count, 2)),
        ],
        compiler_params=pltpu.CompilerParams(vmem_limit_bytes=VMEM_LIMIT),
        name="add",
    )(place, base, *own, *passed)


def local(
    civec, beta_index, beta_sign, alpha_index, alpha_sign, integrals, beta_operator, alpha_operator
):
    classes, pair_count = integrals.shape[:2]
    local_rows, beta_count = civec.shape
    count = lax.axis_size("str")
    blocks = lax.axis_size("blk")
    block_rows = local_rows * count
    window = beta_count * classes // count
    block_at, place = lax.axis_index("blk"), lax.axis_index("str")
    symmetry = place % classes
    partner = jnp.bitwise_xor(block_at, 1 << symmetry)

    def near(array, distance):
        route = [
            (blk * count + at, blk * count + (at ^ distance))
            for blk in range(blocks)
            for at in range(count)
        ]
        return lax.ppermute(array, ("blk", "str"), route)

    def far(array, distance):
        route = [
            (blk * count + at, (blk ^ (1 << at % classes)) * count + (at ^ distance))
            for blk in range(blocks)
            for at in range(count)
        ]
        return lax.ppermute(array, ("blk", "str"), route)

    def one_class(array, start, width):
        return lax.dynamic_slice(array, (symmetry, 0, start), (1, array.shape[1], width))[0]

    def row_codes(index, sign, start, width):
        return one_class(index, start, width) * 4 + one_class(sign, start, width) + 1

    beta_codes = row_codes(beta_index, beta_sign, place // classes * window, window)
    alpha_codes = row_codes(alpha_index, alpha_sign, partner * block_rows, block_rows)
    own_integrals = one_class(integrals, 0, pair_count)
    place = place.astype(jnp.int32).reshape(1)
    codes, kron, rows = prepare(beta_codes, own_integrals, civec)
    later, place = lax.optimization_barrier((civec, place))
    arrived = [near(later if at == 2 else civec, at) for at in range(2, count, 2)]
    codes, alpha_codes, arrived[0] = lax.optimization_barrier((codes, alpha_codes, arrived[0]))
    crossed = [near(piece, 1) for piece in [civec] + arrived]
    pieces = [piece for two in zip([rows] + arrived, crossed) for piece in two]

    sent = mixed_pieces(place, pieces, codes, kron, alpha_codes, window)
    own = [far(sent[at], 2 * at) for at in reversed(range(count // 2))][::-1]
    base = plain_terms(place, pieces, alpha_operator, beta_operator)
    own[0], base = lax.optimization_barrier((own[0], base))
    passed = [near(rows, 1) for rows in own]
    return add_terms(place, base, own, passed, classes)


def solution(mesh):
    placed = (P(("blk", "str"), None), P(), P(), P(), P(), P(), P(), P(("blk", "str"), None))
    return jax.shard_map(
        local, mesh=mesh, in_specs=placed, out_specs=P(("blk", "str"), None), check_vma=False
    )
```

```python
import functools

import jax
import jax.numpy as jnp
from jax import lax
from jax.experimental import pallas as pl
from jax.experimental.pallas import tpu as pltpu
from jax.sharding import PartitionSpec as P

QUAD = 4
SPAN = 120.0
SMALLEST = 2.0**-100
SCALE_ROWS = 16
VMEM_LIMIT = 46 * 1024 * 1024


def whole():
    return pl.BlockSpec(memory_space=pltpu.VMEM)


def coded(values):
    largest = jnp.max(jnp.abs(values), axis=(0, 1), keepdims=True)
    scale = (jnp.maximum(largest, SMALLEST) * 1.01).astype(jnp.bfloat16)
    share = jnp.sqrt(jnp.abs(values) * (1.0 / scale.astype(jnp.float32)))
    size = jnp.exp2((share * 2.0 - 1.0) * SPAN)
    return jnp.where(values < 0.0, -size, size).astype(jnp.bfloat16), scale


def decoded(codes, scale):
    codes, scale = codes.astype(jnp.float32), scale.astype(jnp.float32)
    share = jnp.log2(jnp.abs(codes)) * (0.5 / SPAN) + 0.5
    value = share * share * scale
    return jnp.where(codes < 0.0, -value, value)


def any_place():
    return pl.BlockSpec(memory_space=pl.ANY)


def in_hbm():
    return pl.BlockSpec(memory_space=pltpu.HBM)


def prepare_kernel(code_ref, integral_ref, rows_ref, out_ref, kron_ref, copied_ref, arrived):
    pairs, window = code_ref.shape
    quads = window // QUAD
    size = pairs * QUAD
    copy = pltpu.make_async_copy(rows_ref, copied_ref, arrived)
    copy.start()
    codes = code_ref[...]
    for part in range(QUAD):
        out_ref[pl.ds(part, pairs, QUAD), :quads] = codes[:, part * quads : (part + 1) * quads]
    spread = (
        lax.broadcasted_iota(jnp.int32, (size, pairs), 0) // QUAD
        == lax.broadcasted_iota(jnp.int32, (size, pairs), 1)
    ).astype(jnp.bfloat16)
    tall = jnp.dot(spread, integral_ref[...], preferred_element_type=jnp.float32)
    wide = lax.dot_general(
        tall.astype(jnp.bfloat16),
        spread,
        (((1,), (1,)), ((), ())),
        preferred_element_type=jnp.float32,
    )
    row = lax.broadcasted_iota(jnp.int32, (size, size), 0)
    column = lax.broadcasted_iota(jnp.int32, (size, size), 1)
    kron_ref[...] = jnp.where(row % QUAD == column % QUAD, wide, 0.0).astype(jnp.bfloat16)
    copy.wait()


def prepare(codes, integrals, rows):
    pairs = codes.shape[0]
    size = pairs * QUAD
    return pl.pallas_call(
        prepare_kernel,
        out_shape=[
            jax.ShapeDtypeStruct((size, 128), jnp.int32),
            jax.ShapeDtypeStruct((size, size), jnp.bfloat16),
            jax.ShapeDtypeStruct(rows.shape, rows.dtype),
        ],
        in_specs=[whole(), whole(), any_place()],
        out_specs=[whole(), whole(), any_place()],
        scratch_shapes=[pltpu.SemaphoreType.DMA],
        compiler_params=pltpu.CompilerParams(vmem_limit_bytes=VMEM_LIMIT),
        cost_estimate=pl.CostEstimate(
            flops=0, bytes_accessed=4 * 1024 * 1024, transcendentals=0
        ),
        name="prepare",
    )(codes, integrals, rows)


def pair_images(first_quad, quads, code_ref, kron_ref, turned):
    beta_count, rows = turned.shape
    size = kron_ref.shape[0]
    halves = size // (2 * QUAD)
    codes = jnp.concatenate(
        [
            jnp.broadcast_to(code_ref[:, quad : quad + 1], (size, 128))
            for quad in range(first_quad, first_quad + quads)
        ],
        axis=0,
    )
    target = jnp.right_shift(codes, 2).astype(jnp.int16)
    value = ((codes & 3) - 1).astype(jnp.float32).astype(jnp.bfloat16)
    lane = lax.broadcasted_iota(jnp.int32, codes.shape, 1).astype(jnp.int16)
    onehot = jnp.concatenate(
        [
            jnp.where(lane == target - jnp.int16(start), value, jnp.zeros((), jnp.bfloat16))
            for start in range(0, beta_count, 128)
        ],
        axis=1,
    )
    coupled = jnp.dot(onehot, turned[...], preferred_element_type=jnp.float32)
    coupled = coupled.astype(jnp.bfloat16)
    low = lax.broadcasted_iota(jnp.int32, (halves, 8, rows), 1) < QUAD
    evens, odds = [], []
    for pair in range(quads // 2):
        first, second = [
            jnp.dot(
                kron_ref[...],
                coupled[at * size : (at + 1) * size],
                preferred_element_type=jnp.float32,
            ).reshape(halves, 8, rows)
            for at in (2 * pair, 2 * pair + 1)
        ]
        evens.append(jnp.where(low, first, pltpu.roll(second, QUAD, 1)))
        odds.append(jnp.where(low, pltpu.roll(first, QUAD, 1), second))
    return [jnp.concatenate(side, axis=1).astype(jnp.bfloat16) for side in (evens, odds)]


def mixed_kernel(count, quads, bundle, place_ref, *refs):
    pieces = refs[:count]
    code_ref, kron_ref, alpha_ref = refs[count : count + 3]
    outs = refs[count + 3 : count + 3 + count // 2]
    rest = refs[count + 3 + count // 2 :]
    held, turned, images, total, lanes, ordered, indices, signs, arrived = rest
    local_rows = pieces[0].shape[0]
    halves, _, window, block_rows = images.shape
    columns = quads * QUAD

    copies = [
        pltpu.make_async_copy(
            pieces[at], held.at[pl.ds(at * local_rows, local_rows)], arrived.at[at]
        )
        for at in range(count)
    ]
    for copy in copies:
        copy.start()
    for start in range(0, block_rows, 128):
        for copy in copies[start // local_rows : (start + 128) // local_rows]:
            copy.wait()
        turned[:, start : start + 128] = held[start : start + 128, :].T

    for start in range(0, window, columns):
        even, odd = pair_images(start // QUAD, quads, code_ref, kron_ref, turned)
        images[:, 0, start : start + columns, :] = even
        images[:, 1, start : start + columns, :] = odd

    indices[...] = jnp.right_shift(alpha_ref[...], 2)
    signs[...] = ((alpha_ref[...] & 3) - 1).astype(jnp.float32)
    position = lax.broadcasted_iota(jnp.int32, (block_rows, block_rows), 0)
    position = jnp.bitwise_xor(position, place_ref[0] * local_rows).astype(jnp.int16)
    total[...] = jnp.zeros_like(total)

    def body(at, carry):
        term = None
        for offset in range(bundle):
            pair = bundle * at + offset
            selector = jnp.where(
                position == indices[pl.ds(pair, 1), :].astype(jnp.int16),
                signs[pl.ds(pair, 1), :].astype(jnp.bfloat16),
                jnp.zeros((), jnp.bfloat16),
            )
            part = jnp.dot(
                images[lax.div(pair, 2), lax.rem(pair, 2)],
                selector,
                preferred_element_type=jnp.float32,
            )
            term = part if term is None else term + part
        total[...] += term
        return carry

    lax.fori_loop(0, 2 * halves // bundle, body, 0)
    codes, scale = coded(total[...])
    total[...] = codes.astype(jnp.float32)
    quad_count = window // QUAD
    for at in range(block_rows // 128):
        rows = slice(at * 128, (at + 1) * 128)
        lanes[at] = total[:, rows]
        ordered[rows, :] = jnp.concatenate(
            [lanes[at, pl.ds(part, quad_count, QUAD), :] for part in range(QUAD)], axis=0
        ).T.astype(jnp.bfloat16)
    for at in range(count // 2):
        outs[at][2 * local_rows :, :] = jnp.broadcast_to(scale, (SCALE_ROWS, window))
    for at in range(count):
        start = pl.multiple_of((place_ref[0] ^ at) * local_rows, local_rows)
        rows = slice(at % 2 * local_rows, (at % 2 + 1) * local_rows)
        outs[at // 2][rows, :] = ordered[pl.ds(start, local_rows), :]


def mixed_pieces(place, pieces, codes, kron, alpha_codes, window):
    count = len(pieces)
    local_rows, beta_count = pieces[0].shape
    pairs, block_rows = alpha_codes.shape
    bundle = next(size for size in (25, 10, 5, 2, 1) if pairs % size == 0)
    quads = min(8, window // QUAD, 8 * 512 // block_rows)
    flops = 2 * window * pairs * block_rows * (beta_count + pairs * QUAD + block_rows)
    return pl.pallas_call(
        functools.partial(mixed_kernel, count, quads, bundle),
        out_shape=[jax.ShapeDtypeStruct((2 * local_rows + SCALE_ROWS, window), jnp.bfloat16)]
        * (count // 2),
        in_specs=[pl.BlockSpec(memory_space=pltpu.SMEM)]
        + [any_place()] * count
        + [whole()] * 3,
        out_specs=[whole()] * (count // 2),
        scratch_shapes=[
            pltpu.VMEM((block_rows, beta_count), jnp.bfloat16),
            pltpu.VMEM((beta_count, block_rows), jnp.bfloat16),
            pltpu.VMEM((pairs // 2, 2, window, block_rows), jnp.bfloat16),
            pltpu.VMEM((window, block_rows), jnp.float32),
            pltpu.VMEM((block_rows // 128, window, 128), jnp.float32),
            pltpu.VMEM((block_rows, window), jnp.bfloat16),
            pltpu.VMEM((pairs, block_rows), jnp.int32),
            pltpu.VMEM((pairs, block_rows), jnp.float32),
            pltpu.SemaphoreType.DMA((count,)),
        ],
        compiler_params=pltpu.CompilerParams(vmem_limit_bytes=VMEM_LIMIT),
        cost_estimate=pl.CostEstimate(flops=flops, bytes_accessed=1 << 20, transcendentals=0),
        name="mixed",
    )(place, *pieces, codes, kron, alpha_codes)


def plain_kernel(count, place_ref, *refs):
    pieces = refs[:count]
    alpha_source, beta_source, out_ref, block, alpha_ref, beta_ref, arrived = refs[count:]
    local_rows = pieces[0].shape[0]
    copies = [
        pltpu.make_async_copy(alpha_source, alpha_ref, arrived.at[count]),
        pltpu.make_async_copy(beta_source, beta_ref, arrived.at[count + 1]),
    ]
    for at in range(count):
        start = pl.multiple_of((place_ref[0] ^ at) * local_rows, local_rows)
        copies.append(
            pltpu.make_async_copy(
                pieces[at], block.at[pl.ds(start, local_rows)], arrived.at[at]
            )
        )
    for copy in copies:
        copy.start()
    for copy in copies:
        copy.wait()
    start = pl.multiple_of(place_ref[0] * local_rows, local_rows)
    out_ref[...] = jnp.dot(
        alpha_ref[...], block[...], preferred_element_type=jnp.float32
    ) + jnp.dot(
        block[pl.ds(start, local_rows), :], beta_ref[...], preferred_element_type=jnp.float32
    )


def plain_terms(place, pieces, alpha_operator, beta_operator):
    count = len(pieces)
    local_rows, beta_count = pieces[0].shape
    block_rows = alpha_operator.shape[1]
    return pl.pallas_call(
        functools.partial(plain_kernel, count),
        out_shape=jax.ShapeDtypeStruct((local_rows, beta_count), jnp.float32),
        in_specs=[pl.BlockSpec(memory_space=pltpu.SMEM)]
        + [any_place()] * count
        + [in_hbm(), in_hbm()],
        out_specs=whole(),
        scratch_shapes=[
            pltpu.VMEM((block_rows, beta_count), jnp.bfloat16),
            pltpu.VMEM(alpha_operator.shape, jnp.bfloat16),
            pltpu.VMEM(beta_operator.shape, jnp.bfloat16),
            pltpu.SemaphoreType.DMA((count + 2,)),
        ],
        compiler_params=pltpu.CompilerParams(vmem_limit_bytes=VMEM_LIMIT),
        cost_estimate=pl.CostEstimate(
            flops=2 * local_rows * beta_count * (beta_count + block_rows),
            bytes_accessed=2 * beta_count * (beta_count + block_rows),
            transcendentals=0,
        ),
        name="plain",
    )(place, *pieces, alpha_operator, beta_operator)


def add_kernel(count, classes, place_ref, base_ref, *refs):
    own, passed = refs[:count], refs[count : 2 * count]
    out_ref, held, scales, arrived = refs[2 * count :]
    local_rows, window = held.shape[1:]
    copies = []
    for at in range(count):
        for side, source in enumerate((own[at], passed[at])):
            slot = 2 * at + side
            rows = source.at[pl.ds(side * local_rows, local_rows)]
            scale = source.at[pl.ds(2 * local_rows, SCALE_ROWS)]
            copies.append(pltpu.make_async_copy(rows, held.at[slot], arrived.at[slot, 0]))
            copies.append(pltpu.make_async_copy(scale, scales.at[slot], arrived.at[slot, 1]))
    for copy in copies:
        copy.start()
    chunk = place_ref[0] // classes
    for at in range(count):
        for copy in copies[4 * at : 4 * at + 4]:
            copy.wait()
        columns = pl.ds(pl.multiple_of((chunk ^ (count - 1 - at)) * window, window), window)
        out_ref[:, columns] = base_ref[:, columns] + (
            decoded(held[2 * at], scales[2 * at, :1, :1])
            + decoded(held[2 * at + 1], scales[2 * at + 1, :1, :1])
        )


def add_terms(place, base, own, passed, classes):
    count = len(own)
    rows, window = own[0].shape
    local_rows = (rows - SCALE_ROWS) // 2
    return pl.pallas_call(
        functools.partial(add_kernel, count, classes),
        out_shape=jax.ShapeDtypeStruct(base.shape, jnp.float32),
        in_specs=[pl.BlockSpec(memory_space=pltpu.SMEM), whole()] + [any_place()] * (2 * count),
        out_specs=whole(),
        scratch_shapes=[
            pltpu.VMEM((2 * count, local_rows, window), jnp.bfloat16),
            pltpu.VMEM((2 * count, SCALE_ROWS, window), jnp.bfloat16),
            pltpu.SemaphoreType.DMA((2 * count, 2)),
        ],
        compiler_params=pltpu.CompilerParams(vmem_limit_bytes=VMEM_LIMIT),
        name="add",
    )(place, base, *own, *passed)


def local(
    civec, beta_index, beta_sign, alpha_index, alpha_sign, integrals, beta_operator, alpha_operator
):
    classes, pair_count = integrals.shape[:2]
    local_rows, beta_count = civec.shape
    count = lax.axis_size("str")
    blocks = lax.axis_size("blk")
    block_rows = local_rows * count
    window = beta_count * classes // count
    block_at, place = lax.axis_index("blk"), lax.axis_index("str")
    symmetry = place % classes
    partner = jnp.bitwise_xor(block_at, 1 << symmetry)

    def near(array, distance):
        route = [
            (blk * count + at, blk * count + (at ^ distance))
            for blk in range(blocks)
            for at in range(count)
        ]
        return lax.ppermute(array, ("blk", "str"), route)

    def far(array, distance):
        route = [
            (blk * count + at, (blk ^ (1 << at % classes)) * count + (at ^ distance))
            for blk in range(blocks)
            for at in range(count)
        ]
        return lax.ppermute(array, ("blk", "str"), route)

    def one_class(array, start, width):
        return lax.dynamic_slice(array, (symmetry, 0, start), (1, array.shape[1], width))[0]

    def row_codes(index, sign, start, width):
        return one_class(index, start, width) * 4 + one_class(sign, start, width) + 1

    beta_codes = row_codes(beta_index, beta_sign, place // classes * window, window)
    alpha_codes = row_codes(alpha_index, alpha_sign, partner * block_rows, block_rows)
    own_integrals = one_class(integrals, 0, pair_count)
    place = place.astype(jnp.int32).reshape(1)
    codes, kron, rows = prepare(beta_codes, own_integrals, civec)
    later, place = lax.optimization_barrier((civec, place))
    arrived = [near(later if at == 2 else civec, at) for at in range(2, count, 2)]
    codes, alpha_codes, arrived[-1] = lax.optimization_barrier((codes, alpha_codes, arrived[-1]))
    crossed = [near(piece, 1) for piece in [civec] + arrived]
    pieces = [piece for two in zip([rows] + arrived, crossed) for piece in two]

    sent = mixed_pieces(place, pieces, codes, kron, alpha_codes, window)
    own = [far(sent[at], 2 * at) for at in reversed(range(count // 2))]
    base = plain_terms(place, pieces, alpha_operator, beta_operator)
    own[0], base = lax.optimization_barrier((own[0], base))
    passed = [near(rows, 1) for rows in own]
    return add_terms(place, base, own, passed, classes)


def solution(mesh):
    placed = (P(("blk", "str"), None), P(), P(), P(), P(), P(), P(), P(("blk", "str"), None))
    return jax.shard_map(
        local, mesh=mesh, in_specs=placed, out_specs=P(("blk", "str"), None), check_vma=False
    )
```

```python
import functools

import jax
import jax.numpy as jnp
from jax import lax
from jax.experimental import pallas as pl
from jax.experimental.pallas import tpu as pltpu
from jax.sharding import PartitionSpec as P

QUAD = 4
SPAN = 120.0
SMALLEST = 2.0**-100
SCALE_ROWS = 16
VMEM_LIMIT = 46 * 1024 * 1024


def whole():
    return pl.BlockSpec(memory_space=pltpu.VMEM)


def coded(values):
    largest = jnp.max(jnp.abs(values), axis=(0, 1), keepdims=True)
    scale = (jnp.maximum(largest, SMALLEST) * 1.01).astype(jnp.bfloat16)
    share = jnp.sqrt(jnp.abs(values) * (1.0 / scale.astype(jnp.float32)))
    size = jnp.exp2((share * 2.0 - 1.0) * SPAN)
    return jnp.where(values < 0.0, -size, size).astype(jnp.bfloat16), scale


def decoded(codes, scale):
    codes, scale = codes.astype(jnp.float32), scale.astype(jnp.float32)
    share = jnp.log2(jnp.abs(codes)) * (0.5 / SPAN) + 0.5
    value = share * share * scale
    return jnp.where(codes < 0.0, -value, value)


def any_place():
    return pl.BlockSpec(memory_space=pl.ANY)


def in_hbm():
    return pl.BlockSpec(memory_space=pltpu.HBM)


def prepare_kernel(code_ref, integral_ref, rows_ref, out_ref, kron_ref, copied_ref, arrived):
    pairs, window = code_ref.shape
    quads = window // QUAD
    size = pairs * QUAD
    copy = pltpu.make_async_copy(rows_ref, copied_ref, arrived)
    copy.start()
    codes = code_ref[...]
    for part in range(QUAD):
        out_ref[pl.ds(part, pairs, QUAD), :quads] = codes[:, part * quads : (part + 1) * quads]
    spread = (
        lax.broadcasted_iota(jnp.int32, (size, pairs), 0) // QUAD
        == lax.broadcasted_iota(jnp.int32, (size, pairs), 1)
    ).astype(jnp.bfloat16)
    tall = jnp.dot(spread, integral_ref[...], preferred_element_type=jnp.float32)
    wide = lax.dot_general(
        tall.astype(jnp.bfloat16),
        spread,
        (((1,), (1,)), ((), ())),
        preferred_element_type=jnp.float32,
    )
    row = lax.broadcasted_iota(jnp.int32, (size, size), 0)
    column = lax.broadcasted_iota(jnp.int32, (size, size), 1)
    kron_ref[...] = jnp.where(row % QUAD == column % QUAD, wide, 0.0).astype(jnp.bfloat16)
    copy.wait()


def prepare(codes, integrals, rows):
    pairs = codes.shape[0]
    size = pairs * QUAD
    return pl.pallas_call(
        prepare_kernel,
        out_shape=[
            jax.ShapeDtypeStruct((size, 128), jnp.int32),
            jax.ShapeDtypeStruct((size, size), jnp.bfloat16),
            jax.ShapeDtypeStruct(rows.shape, rows.dtype),
        ],
        in_specs=[whole(), whole(), any_place()],
        out_specs=[whole(), whole(), any_place()],
        scratch_shapes=[pltpu.SemaphoreType.DMA],
        compiler_params=pltpu.CompilerParams(vmem_limit_bytes=VMEM_LIMIT),
        cost_estimate=pl.CostEstimate(
            flops=0, bytes_accessed=4 * 1024 * 1024, transcendentals=0
        ),
        name="prepare",
    )(codes, integrals, rows)


def pair_images(first_quad, quads, code_ref, kron_ref, turned):
    beta_count, rows = turned.shape
    size = kron_ref.shape[0]
    halves = size // (2 * QUAD)
    codes = jnp.concatenate(
        [
            jnp.broadcast_to(code_ref[:, quad : quad + 1], (size, 128))
            for quad in range(first_quad, first_quad + quads)
        ],
        axis=0,
    )
    target = jnp.right_shift(codes, 2).astype(jnp.int16)
    value = ((codes & 3) - 1).astype(jnp.float32).astype(jnp.bfloat16)
    lane = lax.broadcasted_iota(jnp.int32, codes.shape, 1).astype(jnp.int16)
    onehot = jnp.concatenate(
        [
            jnp.where(lane == target - jnp.int16(start), value, jnp.zeros((), jnp.bfloat16))
            for start in range(0, beta_count, 128)
        ],
        axis=1,
    )
    coupled = jnp.dot(onehot, turned[...], preferred_element_type=jnp.float32)
    coupled = coupled.astype(jnp.bfloat16)
    low = lax.broadcasted_iota(jnp.int32, (halves, 8, rows), 1) < QUAD
    evens, odds = [], []
    for pair in range(quads // 2):
        first, second = [
            jnp.dot(
                kron_ref[...],
                coupled[at * size : (at + 1) * size],
                preferred_element_type=jnp.float32,
            ).reshape(halves, 8, rows)
            for at in (2 * pair, 2 * pair + 1)
        ]
        evens.append(jnp.where(low, first, pltpu.roll(second, QUAD, 1)))
        odds.append(jnp.where(low, pltpu.roll(first, QUAD, 1), second))
    return [jnp.concatenate(side, axis=1).astype(jnp.bfloat16) for side in (evens, odds)]


def mixed_kernel(count, quads, place_ref, *refs):
    pieces = refs[:count]
    code_ref, kron_ref, alpha_ref = refs[count : count + 3]
    outs = refs[count + 3 : count + 3 + count // 2]
    rest = refs[count + 3 + count // 2 :]
    held, turned, images, total, lanes, ordered, indices, signs, arrived = rest
    local_rows = pieces[0].shape[0]
    halves, _, window, block_rows = images.shape
    columns = quads * QUAD

    copies = [
        pltpu.make_async_copy(
            pieces[at], held.at[pl.ds(at * local_rows, local_rows)], arrived.at[at]
        )
        for at in range(count)
    ]
    for copy in copies:
        copy.start()
    for start in range(0, block_rows, 128):
        for copy in copies[start // local_rows : (start + 128) // local_rows]:
            copy.wait()
        turned[:, start : start + 128] = held[start : start + 128, :].T

    for start in range(0, window, columns):
        even, odd = pair_images(start // QUAD, quads, code_ref, kron_ref, turned)
        images[:, 0, start : start + columns, :] = even
        images[:, 1, start : start + columns, :] = odd

    indices[...] = jnp.right_shift(alpha_ref[...], 2)
    signs[...] = ((alpha_ref[...] & 3) - 1).astype(jnp.float32)
    position = lax.broadcasted_iota(jnp.int32, (block_rows, block_rows), 0)
    position = jnp.bitwise_xor(position, place_ref[0] * local_rows).astype(jnp.int16)
    term = None
    for pair in range(2 * halves):
        selector = jnp.where(
            position == indices[pair : pair + 1, :].astype(jnp.int16),
            signs[pair : pair + 1, :].astype(jnp.bfloat16),
            jnp.zeros((), jnp.bfloat16),
        )
        part = jnp.dot(
            images[pair // 2, pair % 2], selector, preferred_element_type=jnp.float32
        )
        term = part if term is None else term + part
    codes, scale = coded(term)
    total[...] = codes.astype(jnp.float32)
    quad_count = window // QUAD
    for at in range(block_rows // 128):
        rows = slice(at * 128, (at + 1) * 128)
        lanes[at] = total[:, rows]
        ordered[rows, :] = jnp.concatenate(
            [lanes[at, pl.ds(part, quad_count, QUAD), :] for part in range(QUAD)], axis=0
        ).T.astype(jnp.bfloat16)
    for at in range(count // 2):
        outs[at][2 * local_rows :, :] = jnp.broadcast_to(scale, (SCALE_ROWS, window))
    for at in range(count):
        start = pl.multiple_of((place_ref[0] ^ at) * local_rows, local_rows)
        rows = slice(at % 2 * local_rows, (at % 2 + 1) * local_rows)
        outs[at // 2][rows, :] = ordered[pl.ds(start, local_rows), :]


def mixed_pieces(place, pieces, codes, kron, alpha_codes, window):
    count = len(pieces)
    local_rows, beta_count = pieces[0].shape
    pairs, block_rows = alpha_codes.shape
    quads = min(8, window // QUAD, 8 * 512 // block_rows)
    flops = 2 * window * pairs * block_rows * (beta_count + pairs * QUAD + block_rows)
    return pl.pallas_call(
        functools.partial(mixed_kernel, count, quads),
        out_shape=[jax.ShapeDtypeStruct((2 * local_rows + SCALE_ROWS, window), jnp.bfloat16)]
        * (count // 2),
        in_specs=[pl.BlockSpec(memory_space=pltpu.SMEM)]
        + [any_place()] * count
        + [whole()] * 3,
        out_specs=[whole()] * (count // 2),
        scratch_shapes=[
            pltpu.VMEM((block_rows, beta_count), jnp.bfloat16),
            pltpu.VMEM((beta_count, block_rows), jnp.bfloat16),
            pltpu.VMEM((pairs // 2, 2, window, block_rows), jnp.bfloat16),
            pltpu.VMEM((window, block_rows), jnp.float32),
            pltpu.VMEM((block_rows // 128, window, 128), jnp.float32),
            pltpu.VMEM((block_rows, window), jnp.bfloat16),
            pltpu.VMEM((pairs, block_rows), jnp.int32),
            pltpu.VMEM((pairs, block_rows), jnp.float32),
            pltpu.SemaphoreType.DMA((count,)),
        ],
        compiler_params=pltpu.CompilerParams(vmem_limit_bytes=VMEM_LIMIT),
        cost_estimate=pl.CostEstimate(flops=flops, bytes_accessed=1 << 20, transcendentals=0),
        name="mixed",
    )(place, *pieces, codes, kron, alpha_codes)


def plain_kernel(count, place_ref, *refs):
    pieces = refs[:count]
    alpha_source, beta_source, out_ref, block, alpha_ref, beta_ref, arrived = refs[count:]
    local_rows = pieces[0].shape[0]
    copies = [
        pltpu.make_async_copy(alpha_source, alpha_ref, arrived.at[count]),
        pltpu.make_async_copy(beta_source, beta_ref, arrived.at[count + 1]),
    ]
    for at in range(count):
        start = pl.multiple_of((place_ref[0] ^ at) * local_rows, local_rows)
        copies.append(
            pltpu.make_async_copy(
                pieces[at], block.at[pl.ds(start, local_rows)], arrived.at[at]
            )
        )
    for copy in copies:
        copy.start()
    for copy in copies:
        copy.wait()
    start = pl.multiple_of(place_ref[0] * local_rows, local_rows)
    out_ref[...] = jnp.dot(
        alpha_ref[...], block[...], preferred_element_type=jnp.float32
    ) + jnp.dot(
        block[pl.ds(start, local_rows), :], beta_ref[...], preferred_element_type=jnp.float32
    )


def plain_terms(place, pieces, alpha_operator, beta_operator):
    count = len(pieces)
    local_rows, beta_count = pieces[0].shape
    block_rows = alpha_operator.shape[1]
    return pl.pallas_call(
        functools.partial(plain_kernel, count),
        out_shape=jax.ShapeDtypeStruct((local_rows, beta_count), jnp.float32),
        in_specs=[pl.BlockSpec(memory_space=pltpu.SMEM)]
        + [any_place()] * count
        + [in_hbm(), in_hbm()],
        out_specs=whole(),
        scratch_shapes=[
            pltpu.VMEM((block_rows, beta_count), jnp.bfloat16),
            pltpu.VMEM(alpha_operator.shape, jnp.bfloat16),
            pltpu.VMEM(beta_operator.shape, jnp.bfloat16),
            pltpu.SemaphoreType.DMA((count + 2,)),
        ],
        compiler_params=pltpu.CompilerParams(vmem_limit_bytes=VMEM_LIMIT),
        cost_estimate=pl.CostEstimate(
            flops=2 * local_rows * beta_count * (beta_count + block_rows),
            bytes_accessed=2 * beta_count * (beta_count + block_rows),
            transcendentals=0,
        ),
        name="plain",
    )(place, *pieces, alpha_operator, beta_operator)


def add_kernel(count, classes, place_ref, base_ref, *refs):
    own, passed = refs[:count], refs[count : 2 * count]
    out_ref, held, scales, arrived = refs[2 * count :]
    local_rows, window = held.shape[1:]
    copies = []
    for at in range(count):
        for side, source in enumerate((own[at], passed[at])):
            slot = 2 * at + side
            rows = source.at[pl.ds(side * local_rows, local_rows)]
            scale = source.at[pl.ds(2 * local_rows, SCALE_ROWS)]
            copies.append(pltpu.make_async_copy(rows, held.at[slot], arrived.at[slot, 0]))
            copies.append(pltpu.make_async_copy(scale, scales.at[slot], arrived.at[slot, 1]))
    for copy in copies:
        copy.start()
    chunk = place_ref[0] // classes
    for at in range(count):
        for copy in copies[4 * at : 4 * at + 4]:
            copy.wait()
        columns = pl.ds(pl.multiple_of((chunk ^ (count - 1 - at)) * window, window), window)
        out_ref[:, columns] = base_ref[:, columns] + (
            decoded(held[2 * at], scales[2 * at, :1, :1])
            + decoded(held[2 * at + 1], scales[2 * at + 1, :1, :1])
        )


def add_terms(place, base, own, passed, classes):
    count = len(own)
    rows, window = own[0].shape
    local_rows = (rows - SCALE_ROWS) // 2
    return pl.pallas_call(
        functools.partial(add_kernel, count, classes),
        out_shape=jax.ShapeDtypeStruct(base.shape, jnp.float32),
        in_specs=[pl.BlockSpec(memory_space=pltpu.SMEM), whole()] + [any_place()] * (2 * count),
        out_specs=whole(),
        scratch_shapes=[
            pltpu.VMEM((2 * count, local_rows, window), jnp.bfloat16),
            pltpu.VMEM((2 * count, SCALE_ROWS, window), jnp.bfloat16),
            pltpu.SemaphoreType.DMA((2 * count, 2)),
        ],
        compiler_params=pltpu.CompilerParams(vmem_limit_bytes=VMEM_LIMIT),
        name="add",
    )(place, base, *own, *passed)


def local(
    civec, beta_index, beta_sign, alpha_index, alpha_sign, integrals, beta_operator, alpha_operator
):
    classes, pair_count = integrals.shape[:2]
    local_rows, beta_count = civec.shape
    count = lax.axis_size("str")
    blocks = lax.axis_size("blk")
    block_rows = local_rows * count
    window = beta_count * classes // count
    block_at, place = lax.axis_index("blk"), lax.axis_index("str")
    symmetry = place % classes
    partner = jnp.bitwise_xor(block_at, 1 << symmetry)

    def near(array, distance):
        route = [
            (blk * count + at, blk * count + (at ^ distance))
            for blk in range(blocks)
            for at in range(count)
        ]
        return lax.ppermute(array, ("blk", "str"), route)

    def far(array, distance):
        route = [
            (blk * count + at, (blk ^ (1 << at % classes)) * count + (at ^ distance))
            for blk in range(blocks)
            for at in range(count)
        ]
        return lax.ppermute(array, ("blk", "str"), route)

    def one_class(array, start, width):
        return lax.dynamic_slice(array, (symmetry, 0, start), (1, array.shape[1], width))[0]

    def row_codes(index, sign, start, width):
        return one_class(index, start, width) * 4 + one_class(sign, start, width) + 1

    beta_codes = row_codes(beta_index, beta_sign, place // classes * window, window)
    alpha_codes = row_codes(alpha_index, alpha_sign, partner * block_rows, block_rows)
    own_integrals = one_class(integrals, 0, pair_count)
    place = place.astype(jnp.int32).reshape(1)
    codes, kron, rows = prepare(beta_codes, own_integrals, civec)
    later, place = lax.optimization_barrier((civec, place))
    arrived = [near(later if at == 2 else civec, at) for at in range(2, count, 2)]
    codes, alpha_codes, arrived[-1] = lax.optimization_barrier((codes, alpha_codes, arrived[-1]))
    crossed = [near(piece, 1) for piece in [civec] + arrived]
    pieces = [piece for two in zip([rows] + arrived, crossed) for piece in two]

    sent = mixed_pieces(place, pieces, codes, kron, alpha_codes, window)
    own = [far(sent[at], 2 * at) for at in reversed(range(count // 2))]
    base = plain_terms(place, pieces, alpha_operator, beta_operator)
    own[0], base = lax.optimization_barrier((own[0], base))
    passed = [near(rows, 1) for rows in own]
    return add_terms(place, base, own, passed, classes)


def solution(mesh):
    placed = (P(("blk", "str"), None), P(), P(), P(), P(), P(), P(), P(("blk", "str"), None))
    return jax.shard_map(
        local, mesh=mesh, in_specs=placed, out_specs=P(("blk", "str"), None), check_vma=False
    )
```

```python
import functools

import jax
import jax.numpy as jnp
from jax import lax
from jax.experimental import pallas as pl
from jax.experimental.pallas import tpu as pltpu
from jax.sharding import PartitionSpec as P

QUAD = 4
SPAN = 120.0
SMALLEST = 2.0**-100
SCALE_ROWS = 16
VMEM_LIMIT = 46 * 1024 * 1024


def whole():
    return pl.BlockSpec(memory_space=pltpu.VMEM)


def coded(values):
    largest = jnp.max(jnp.abs(values), axis=(0, 1), keepdims=True)
    scale = (jnp.maximum(largest, SMALLEST) * 1.01).astype(jnp.bfloat16)
    share = jnp.sqrt(jnp.abs(values) * (1.0 / scale.astype(jnp.float32)))
    size = jnp.exp2((share * 2.0 - 1.0) * SPAN)
    return jnp.where(values < 0.0, -size, size).astype(jnp.bfloat16), scale


def decoded(codes, scale):
    codes, scale = codes.astype(jnp.float32), scale.astype(jnp.float32)
    share = jnp.log2(jnp.abs(codes)) * (0.5 / SPAN) + 0.5
    value = share * share * scale
    return jnp.where(codes < 0.0, -value, value)


def any_place():
    return pl.BlockSpec(memory_space=pl.ANY)


def in_hbm():
    return pl.BlockSpec(memory_space=pltpu.HBM)


def prepare_kernel(code_ref, integral_ref, rows_ref, out_ref, kron_ref, copied_ref, arrived):
    pairs, window = code_ref.shape
    quads = window // QUAD
    size = pairs * QUAD
    copy = pltpu.make_async_copy(rows_ref, copied_ref, arrived)
    copy.start()
    codes = code_ref[...]
    for part in range(QUAD):
        out_ref[pl.ds(part, pairs, QUAD), :quads] = codes[:, part * quads : (part + 1) * quads]
    spread = (
        lax.broadcasted_iota(jnp.int32, (size, pairs), 0) // QUAD
        == lax.broadcasted_iota(jnp.int32, (size, pairs), 1)
    ).astype(jnp.bfloat16)
    tall = jnp.dot(spread, integral_ref[...], preferred_element_type=jnp.float32)
    wide = lax.dot_general(
        tall.astype(jnp.bfloat16),
        spread,
        (((1,), (1,)), ((), ())),
        preferred_element_type=jnp.float32,
    )
    row = lax.broadcasted_iota(jnp.int32, (size, size), 0)
    column = lax.broadcasted_iota(jnp.int32, (size, size), 1)
    kron_ref[...] = jnp.where(row % QUAD == column % QUAD, wide, 0.0).astype(jnp.bfloat16)
    copy.wait()


def prepare(codes, integrals, rows):
    pairs = codes.shape[0]
    size = pairs * QUAD
    return pl.pallas_call(
        prepare_kernel,
        out_shape=[
            jax.ShapeDtypeStruct((size, 128), jnp.int32),
            jax.ShapeDtypeStruct((size, size), jnp.bfloat16),
            jax.ShapeDtypeStruct(rows.shape, rows.dtype),
        ],
        in_specs=[whole(), whole(), any_place()],
        out_specs=[whole(), whole(), any_place()],
        scratch_shapes=[pltpu.SemaphoreType.DMA],
        compiler_params=pltpu.CompilerParams(vmem_limit_bytes=VMEM_LIMIT),
        cost_estimate=pl.CostEstimate(
            flops=0, bytes_accessed=4 * 1024 * 1024, transcendentals=0
        ),
        name="prepare",
    )(codes, integrals, rows)


def pair_images(first_quad, quads, code_ref, kron_ref, turned):
    beta_count, rows = turned.shape
    size = kron_ref.shape[0]
    halves = size // (2 * QUAD)
    codes = jnp.concatenate(
        [
            jnp.broadcast_to(code_ref[:, quad : quad + 1], (size, 128))
            for quad in range(first_quad, first_quad + quads)
        ],
        axis=0,
    )
    target = jnp.right_shift(codes, 2).astype(jnp.int16)
    value = ((codes & 3) - 1).astype(jnp.float32).astype(jnp.bfloat16)
    lane = lax.broadcasted_iota(jnp.int32, codes.shape, 1).astype(jnp.int16)
    onehot = jnp.concatenate(
        [
            jnp.where(lane == target - jnp.int16(start), value, jnp.zeros((), jnp.bfloat16))
            for start in range(0, beta_count, 128)
        ],
        axis=1,
    )
    coupled = jnp.dot(onehot, turned[...], preferred_element_type=jnp.float32)
    coupled = coupled.astype(jnp.bfloat16)
    low = lax.broadcasted_iota(jnp.int32, (halves, 8, rows), 1) < QUAD
    evens, odds = [], []
    for pair in range(quads // 2):
        first, second = [
            jnp.dot(
                kron_ref[...],
                coupled[at * size : (at + 1) * size],
                preferred_element_type=jnp.float32,
            ).reshape(halves, 8, rows)
            for at in (2 * pair, 2 * pair + 1)
        ]
        evens.append(jnp.where(low, first, pltpu.roll(second, QUAD, 1)))
        odds.append(jnp.where(low, pltpu.roll(first, QUAD, 1), second))
    return [jnp.concatenate(side, axis=1).astype(jnp.bfloat16) for side in (evens, odds)]


def mixed_kernel(count, quads, place_ref, *refs):
    pieces = refs[:count]
    code_ref, kron_ref, alpha_ref = refs[count : count + 3]
    outs = refs[count + 3 : count + 3 + count // 2]
    rest = refs[count + 3 + count // 2 :]
    held, turned, images, total, lanes, ordered, indices, signs, arrived = rest
    local_rows = pieces[0].shape[0]
    halves, _, window, block_rows = images.shape
    columns = quads * QUAD

    copies = [
        pltpu.make_async_copy(
            pieces[at], held.at[pl.ds(at * local_rows, local_rows)], arrived.at[at]
        )
        for at in range(count)
    ]
    for copy in copies:
        copy.start()
    for start in range(0, block_rows, 128):
        for copy in copies[start // local_rows : (start + 128) // local_rows]:
            copy.wait()
        turned[:, start : start + 128] = held[start : start + 128, :].T

    for start in range(0, window, columns):
        even, odd = pair_images(start // QUAD, quads, code_ref, kron_ref, turned)
        images[:, 0, start : start + columns, :] = even
        images[:, 1, start : start + columns, :] = odd

    indices[...] = jnp.right_shift(alpha_ref[...], 2)
    signs[...] = ((alpha_ref[...] & 3) - 1).astype(jnp.float32)
    position = lax.broadcasted_iota(jnp.int32, (block_rows, block_rows), 0)
    position = jnp.bitwise_xor(position, place_ref[0] * local_rows).astype(jnp.int16)
    term = None
    for pair in range(2 * halves):
        selector = jnp.where(
            position == indices[pair : pair + 1, :].astype(jnp.int16),
            signs[pair : pair + 1, :].astype(jnp.bfloat16),
            jnp.zeros((), jnp.bfloat16),
        )
        part = jnp.dot(
            images[pair // 2, pair % 2], selector, preferred_element_type=jnp.float32
        )
        term = part if term is None else term + part
    codes, scale = coded(term)
    total[...] = codes.astype(jnp.float32)
    quad_count = window // QUAD
    for at in range(block_rows // 128):
        rows = slice(at * 128, (at + 1) * 128)
        lanes[at] = total[:, rows]
        ordered[rows, :] = jnp.concatenate(
            [lanes[at, pl.ds(part, quad_count, QUAD), :] for part in range(QUAD)], axis=0
        ).T.astype(jnp.bfloat16)
    for at in range(count // 2):
        outs[at][2 * local_rows :, :] = jnp.broadcast_to(scale, (SCALE_ROWS, window))
    for at in range(count):
        start = pl.multiple_of((place_ref[0] ^ at) * local_rows, local_rows)
        rows = slice(at % 2 * local_rows, (at % 2 + 1) * local_rows)
        outs[at // 2][rows, :] = ordered[pl.ds(start, local_rows), :]


def mixed_pieces(place, pieces, codes, kron, alpha_codes, window):
    count = len(pieces)
    local_rows, beta_count = pieces[0].shape
    pairs, block_rows = alpha_codes.shape
    quads = min(8, window // QUAD, 8 * 512 // block_rows)
    flops = 2 * window * pairs * block_rows * (beta_count + pairs * QUAD + block_rows)
    return pl.pallas_call(
        functools.partial(mixed_kernel, count, quads),
        out_shape=[jax.ShapeDtypeStruct((2 * local_rows + SCALE_ROWS, window), jnp.bfloat16)]
        * (count // 2),
        in_specs=[pl.BlockSpec(memory_space=pltpu.SMEM)]
        + [any_place()] * count
        + [whole()] * 3,
        out_specs=[whole()] * (count // 2),
        scratch_shapes=[
            pltpu.VMEM((block_rows, beta_count), jnp.bfloat16),
            pltpu.VMEM((beta_count, block_rows), jnp.bfloat16),
            pltpu.VMEM((pairs // 2, 2, window, block_rows), jnp.bfloat16),
            pltpu.VMEM((window, block_rows), jnp.float32),
            pltpu.VMEM((block_rows // 128, window, 128), jnp.float32),
            pltpu.VMEM((block_rows, window), jnp.bfloat16),
            pltpu.VMEM((pairs, block_rows), jnp.int32),
            pltpu.VMEM((pairs, block_rows), jnp.float32),
            pltpu.SemaphoreType.DMA((count,)),
        ],
        compiler_params=pltpu.CompilerParams(vmem_limit_bytes=VMEM_LIMIT),
        cost_estimate=pl.CostEstimate(flops=flops, bytes_accessed=1 << 20, transcendentals=0),
        name="mixed",
    )(place, *pieces, codes, kron, alpha_codes)


def plain_kernel(count, place_ref, *refs):
    pieces = refs[:count]
    alpha_source, beta_source, out_ref, block, alpha_ref, beta_ref, arrived = refs[count:]
    local_rows = pieces[0].shape[0]
    copies = [
        pltpu.make_async_copy(alpha_source, alpha_ref, arrived.at[count]),
        pltpu.make_async_copy(beta_source, beta_ref, arrived.at[count + 1]),
    ]
    for at in range(count):
        start = pl.multiple_of((place_ref[0] ^ at) * local_rows, local_rows)
        copies.append(
            pltpu.make_async_copy(
                pieces[at], block.at[pl.ds(start, local_rows)], arrived.at[at]
            )
        )
    for copy in copies:
        copy.start()
    for copy in copies:
        copy.wait()
    start = pl.multiple_of(place_ref[0] * local_rows, local_rows)
    out_ref[...] = jnp.dot(
        alpha_ref[...], block[...], preferred_element_type=jnp.float32
    ) + jnp.dot(
        block[pl.ds(start, local_rows), :], beta_ref[...], preferred_element_type=jnp.float32
    )


def plain_terms(place, pieces, alpha_operator, beta_operator):
    count = len(pieces)
    local_rows, beta_count = pieces[0].shape
    block_rows = alpha_operator.shape[1]
    return pl.pallas_call(
        functools.partial(plain_kernel, count),
        out_shape=jax.ShapeDtypeStruct((local_rows, beta_count), jnp.float32),
        in_specs=[pl.BlockSpec(memory_space=pltpu.SMEM)]
        + [any_place()] * count
        + [in_hbm(), in_hbm()],
        out_specs=whole(),
        scratch_shapes=[
            pltpu.VMEM((block_rows, beta_count), jnp.bfloat16),
            pltpu.VMEM(alpha_operator.shape, jnp.bfloat16),
            pltpu.VMEM(beta_operator.shape, jnp.bfloat16),
            pltpu.SemaphoreType.DMA((count + 2,)),
        ],
        compiler_params=pltpu.CompilerParams(vmem_limit_bytes=VMEM_LIMIT),
        cost_estimate=pl.CostEstimate(
            flops=2 * local_rows * beta_count * (beta_count + block_rows),
            bytes_accessed=2 * beta_count * (beta_count + block_rows),
            transcendentals=0,
        ),
        name="plain",
    )(place, *pieces, alpha_operator, beta_operator)


def add_kernel(count, classes, place_ref, base_ref, *refs):
    own, passed = refs[:count], refs[count : 2 * count]
    out_ref, held, scales, arrived = refs[2 * count :]
    local_rows, window = held.shape[1:]
    copies = []
    for at in range(count):
        for side, source in enumerate((own[at], passed[at])):
            slot = 2 * at + side
            rows = source.at[pl.ds(side * local_rows, local_rows)]
            scale = source.at[pl.ds(2 * local_rows, SCALE_ROWS)]
            copies.append(pltpu.make_async_copy(rows, held.at[slot], arrived.at[slot, 0]))
            copies.append(pltpu.make_async_copy(scale, scales.at[slot], arrived.at[slot, 1]))
    for copy in copies:
        copy.start()
    chunk = place_ref[0] // classes
    for at in range(count):
        for copy in copies[4 * at : 4 * at + 4]:
            copy.wait()
        columns = pl.ds(pl.multiple_of((chunk ^ (count - 1 - at)) * window, window), window)
        out_ref[:, columns] = base_ref[:, columns] + (
            decoded(held[2 * at], scales[2 * at, :1, :1])
            + decoded(held[2 * at + 1], scales[2 * at + 1, :1, :1])
        )


def add_terms(place, base, own, passed, classes):
    count = len(own)
    rows, window = own[0].shape
    local_rows = (rows - SCALE_ROWS) // 2
    return pl.pallas_call(
        functools.partial(add_kernel, count, classes),
        out_shape=jax.ShapeDtypeStruct(base.shape, jnp.float32),
        in_specs=[pl.BlockSpec(memory_space=pltpu.SMEM), whole()] + [any_place()] * (2 * count),
        out_specs=whole(),
        scratch_shapes=[
            pltpu.VMEM((2 * count, local_rows, window), jnp.bfloat16),
            pltpu.VMEM((2 * count, SCALE_ROWS, window), jnp.bfloat16),
            pltpu.SemaphoreType.DMA((2 * count, 2)),
        ],
        compiler_params=pltpu.CompilerParams(vmem_limit_bytes=VMEM_LIMIT),
        name="add",
    )(place, base, *own, *passed)


def local(
    civec, beta_index, beta_sign, alpha_index, alpha_sign, integrals, beta_operator, alpha_operator
):
    classes, pair_count = integrals.shape[:2]
    local_rows, beta_count = civec.shape
    count = lax.axis_size("str")
    blocks = lax.axis_size("blk")
    block_rows = local_rows * count
    window = beta_count * classes // count
    block_at, place = lax.axis_index("blk"), lax.axis_index("str")
    symmetry = place % classes
    partner = jnp.bitwise_xor(block_at, 1 << symmetry)

    def near(array, distance):
        route = [
            (blk * count + at, blk * count + (at ^ distance))
            for blk in range(blocks)
            for at in range(count)
        ]
        return lax.ppermute(array, ("blk", "str"), route)

    def far(array, distance):
        route = [
            (blk * count + at, (blk ^ (1 << at % classes)) * count + (at ^ distance))
            for blk in range(blocks)
            for at in range(count)
        ]
        return lax.ppermute(array, ("blk", "str"), route)

    def one_class(array, start, width):
        return lax.dynamic_slice(array, (symmetry, 0, start), (1, array.shape[1], width))[0]

    def row_codes(index, sign, start, width):
        return one_class(index, start, width) * 4 + one_class(sign, start, width) + 1

    beta_codes = row_codes(beta_index, beta_sign, place // classes * window, window)
    alpha_codes = row_codes(alpha_index, alpha_sign, partner * block_rows, block_rows)
    own_integrals = one_class(integrals, 0, pair_count)
    place = place.astype(jnp.int32).reshape(1)
    codes, kron, rows = prepare(beta_codes, own_integrals, civec)
    later, place = lax.optimization_barrier((civec, place))
    arrived = [near(later if at == 2 else civec, at) for at in range(2, count, 2)]
    codes, alpha_codes, arrived[-1] = lax.optimization_barrier((codes, alpha_codes, arrived[-1]))
    crossed = [near(piece, 1) for piece in [civec] + arrived]
    pieces = [piece for two in zip([rows] + arrived, crossed) for piece in two]

    sent = mixed_pieces(place, pieces, codes, kron, alpha_codes, window)
    own = [far(sent[at], 2 * at) for at in reversed(range(count // 2))]
    base = plain_terms(place, pieces, alpha_operator, beta_operator)
    own[-1], base = lax.optimization_barrier((own[-1], base))
    passed = [near(rows, 1) for rows in own]
    return add_terms(place, base, own, passed, classes)


def solution(mesh):
    placed = (P(("blk", "str"), None), P(), P(), P(), P(), P(), P(), P(("blk", "str"), None))
    return jax.shard_map(
        local, mesh=mesh, in_specs=placed, out_specs=P(("blk", "str"), None), check_vma=False
    )
```
